512 devices in a mesh: ep: 32 (over x, y), dp: 16 (over z, core).
Axes of the slice: x: 4, y: 8, z: 8, core: 2. Of those that a mesh axis runs over, the one named last changes fastest.
Arguments:
- tokens: bfloat16 [4096, 7168], P('ep', 'dp'), may hold values from -6 to 6
- routes: int32 [4096, 8], P('ep'), may hold values from 0 to 31, all different within a row; in each aligned block of 128 rows (0 to 127, 128 to 255, ...) at most 64 rows name the same one
- weights_int: int32 [4096, 8], P('ep'), may hold values from 1 to 63
- capacity: int32 [32], replicated, may hold values from 12 to 24, as said below
- spill_size: int32 [32], replicated, may hold values from 1 to 24, as said below
- gate_weight: bfloat16 [32, 7168, 1024], P('ep', 'dp'), may hold values from -0.0625 to 0.0625
- up_weight: bfloat16 [32, 7168, 1024], P('ep', 'dp'), may hold values from -0.0625 to 0.0625
- down_weight: bfloat16 [32, 1024, 7168], P('ep', None, 'dp'), may hold values from -0.1875 to 0.1875
Outputs:
- mixed: bfloat16 [4096, 7168], P('ep', 'dp')
The draws below stay inside these ranges and needn't reach their ends.
Inputs may be any that keep to these rules, and one draw needn't show every extreme that they name: `capacity`: each expert's primary slots; the largest, 24, is taken by some expert in every draw. `spill_size`: each expert's overflow slots; the largest, 24, is taken by some expert in every draw. `routes`: A token names 8 different experts; in each aligned block of 128 tokens no expert is named by more than 64 tokens.
All inputs are finite; a program needn't handle non-finite values.
Results may differ from the reference program's by a relative error of at most 0.012.
Values may be sent and summed in bfloat16 or wider, within the bound.
No kernel may reach another device: no remote copies, remote signals or barrier semaphores. Data moves between devices by JAX's collectives and lax.ppermute only.
A program may use at most 128 MiB of HBM per device.

```python
import math
import jax
import jax.numpy as jnp
import numpy as np
from jax import lax

D = 7168
FF = 1024
EXPERTS = 32
TOP = 8
TOK_DEV = 128
MOST = 64
CAP = 24
SPILL = 24
TOKENS = 4096
N_EP = 32
N_DP = 16


def draw_capacity(key, part):
    key = jax.random.fold_in(key, 5)
    first_key, second_key = jax.random.split(key)
    values = jax.random.randint(first_key, (EXPERTS,), CAP // 2, CAP + 1)
    target = jax.random.randint(second_key, (), 0, EXPERTS)
    return values.at[target].set(CAP).astype(jnp.int32)


def draw_spill_size(key, part):
    key = jax.random.fold_in(key, 9)
    first_key, second_key = jax.random.split(key)
    values = jax.random.randint(first_key, (EXPERTS,), 1, SPILL + 1)
    target = jax.random.randint(second_key, (), 0, EXPERTS)
    return values.at[target].set(SPILL).astype(jnp.int32)


def set_ends(drawn, stream_key, least, high):
    dims = drawn.shape
    place = [jax.random.randint(jax.random.fold_in(stream_key, axis), (), 0, dims[axis]) for axis in range(len(dims))]
    drawn = drawn.at[tuple(place)].set(least)
    longest = dims.index(max(dims))
    place[longest] = (place[longest] + 1) % dims[longest]
    return drawn.at[tuple(place)].set(high)


def block_levels(key, extent, shards, low, high):
    factor_of = 1.0
    for dim, blocks in shards:
        heights = jax.random.uniform(jax.random.fold_in(jax.random.fold_in(key, 6), dim), (blocks,), jnp.float32, low / len(shards), high / len(shards))
        factor_of = factor_of * jnp.repeat(jnp.exp(heights), extent[dim] // blocks).reshape((-1,) + (1,) * (len(extent) - 1 - dim))
    return factor_of


def assign_block(rng, own, number, rows, amount, top, most, slope):
    order = jax.random.permutation(rng, amount)
    crowded, ordinary = load_shares(amount, rows * top, most, slope, True), load_shares(amount, rows * top, most, slope, False)
    places = jnp.arange(amount)

    def named(tallies, turn):
        used = int((tallies > 0).sum())
        fixed = max(1, used // 4)
        shifted = fixed + (places - fixed + turn * (used - fixed)) % max(1, amount - fixed)
        return jnp.zeros((amount,), jnp.int32).at[order[jnp.where(places < fixed, places, shifted)]].set(jnp.asarray(tallies, jnp.int32))

    tallies = jnp.where(number % 4 == 0, named(crowded, number // 4), named(ordinary, number - number // 4 - 1))
    mixed = jax.random.permutation(jax.random.fold_in(own, 3), amount)
    giver, receiver = mixed[0:amount // 2 * 2:2], mixed[1:amount // 2 * 2:2]
    room = jnp.minimum(tallies[giver] - 1, most - tallies[receiver]) // 2
    room = jnp.where((giver == order[0]) | (receiver == order[0]) | (tallies[receiver] == 0), 0, jnp.maximum(room, 0))
    shifted = jax.random.randint(jax.random.fold_in(own, 4), (amount // 2,), 0, 1 << 20) % (room + 1)
    tallies = tallies.at[giver].add(-shifted).at[receiver].add(shifted)
    members = jnp.searchsorted(jnp.cumsum(tallies), jnp.arange(rows * top), side="right").astype(jnp.int32)
    listing = members.reshape(top, rows).T
    listing = listing[jax.random.permutation(jax.random.fold_in(own, 1), rows)]
    turn = jax.random.randint(jax.random.fold_in(own, 2), (rows, 1), 0, top)
    return jnp.take_along_axis(listing, (jnp.arange(top)[None, :] + turn) % top, axis=1)


def load_shares(amount, total, reach, skew, full):
    portions = [(1 << 20) // math.isqrt(grade ** skew) + 1 for grade in range(1, amount + 1)]
    largest = reach if full else min(reach, max(-(-total // amount), total * portions[0] // sum(portions)))
    least = 1 if total - largest >= amount - 1 else 0
    counts, surplus = [largest] + [least] * (amount - 1), total - largest - least * (amount - 1)
    while surplus > 0:
        free = [i for i in range(1, amount) if counts[i] < largest] or [i for i in range(1, amount) if counts[i] < reach]
        pool, budget = sum([portions[i] for i in free]), surplus
        for i in free:
            extra = min(reach - counts[i], max(1, budget * portions[i] // pool), surplus)
            counts[i] = counts[i] + extra
            surplus = surplus - extra
    return np.array(counts)


def bell_draw(key, extent, deviation, limit, cuts=(), kind=jnp.bfloat16):
    factor_of = block_levels(key, extent, cuts, -0.22, 0.18) if cuts else 1.0
    array = jax.random.normal(key, extent, jnp.float32) * deviation * factor_of
    return jnp.minimum(jnp.maximum(array, -limit), limit).astype(kind)


def setup_inputs(seed: int = 0) -> dict:
    splits = jax.random.split(jax.random.key(seed), 9)
    tokens = bell_draw(splits[0], (TOKENS, D), 1.0, 6.0, ((0, 32), (1, 16)))
    routes_keys = jax.random.split(jax.random.fold_in(splits[1], 1), TOKENS // TOK_DEV)
    routes_turns = jax.random.permutation(jax.random.fold_in(splits[1], 3), TOKENS // TOK_DEV)
    routes = jax.vmap(lambda own, number: assign_block(jax.random.fold_in(splits[1], 2), own, number, TOK_DEV, EXPERTS, TOP, MOST, 2))(routes_keys, routes_turns).reshape((TOKENS, TOP))
    weights_int = set_ends(jax.random.randint(splits[2], (TOKENS, TOP), 1, 64), jax.random.fold_in(splits[2], 1), 1, 63).astype(jnp.int32)
    capacity = draw_capacity(jax.random.fold_in(splits[8], 71), 0)
    spill_size = draw_spill_size(jax.random.fold_in(splits[8], 71), 0)
    gate_weight = bell_draw(splits[5], (EXPERTS, D, FF), D ** -0.5, 0.0625, ((0, 32), (1, 16)))
    up_weight = bell_draw(splits[6], (EXPERTS, D, FF), D ** -0.5, 0.0625, ((0, 32), (1, 16)))
    down_weight = bell_draw(splits[7], (EXPERTS, FF, D), FF ** -0.5, 0.1875, ((0, 32), (2, 16)))
    return {"tokens": tokens, "routes": routes, "weights_int": weights_int, "capacity": capacity, "spill_size": spill_size, "gate_weight": gate_weight, "up_weight": up_weight, "down_weight": down_weight}


def reference(tokens, routes, weights_int, capacity, spill_size, gate_weight, up_weight, down_weight):
    experts = capacity.shape[0]
    total = tokens.shape[0]
    features = tokens.shape[1]
    block_cols = features // N_DP
    keep_slots = CAP + SPILL
    slot_count = N_EP * keep_slots
    blocks = routes.reshape(N_EP, TOK_DEV, TOP)
    onehot = (blocks[..., None] == jnp.arange(experts, dtype=jnp.int32)).astype(jnp.int32)
    named_count = jnp.sum(onehot, axis=2)
    before = jnp.cumsum(named_count, axis=1) - named_count
    rank_in = jnp.sum(onehot * before[:, :, None, :], axis=3).reshape(total, TOP)
    limit_each = (capacity + spill_size)[routes]
    kept_mask = rank_in < limit_each
    weight_float = weights_int.astype(jnp.float32)
    shares_of = weight_float / jnp.sum(weight_float, axis=1, keepdims=True)
    source_of = jnp.arange(total, dtype=jnp.int32) // TOK_DEV
    padded = jnp.concatenate([tokens, jnp.zeros((1, features), tokens.dtype)], axis=0)

    def one_expert(carry, expert):
        hit_mask = (routes == expert) & kept_mask
        chosen = jnp.any(hit_mask, axis=1)
        weight_of = jnp.sum(jnp.where(hit_mask, shares_of, 0.0), axis=1)
        rank_here = jnp.sum(jnp.where(hit_mask, rank_in, 0), axis=1)
        slot_of = (source_of * keep_slots + rank_here).astype(jnp.int32)
        target = jnp.where(chosen, slot_of, slot_count).astype(jnp.int32)
        table = jnp.full((slot_count,), total, jnp.int32).at[target].set(jnp.arange(total, dtype=jnp.int32), mode="drop")
        gathered = padded[table].reshape(slot_count, N_DP, block_cols).astype(jnp.float32)
        gate_blocks = gate_weight[expert].reshape(N_DP, block_cols, FF).astype(jnp.float32)
        up_blocks = up_weight[expert].reshape(N_DP, block_cols, FF).astype(jnp.float32)
        gate_parts = jnp.einsum("rnd,ndf->rnf", gathered, gate_blocks)
        up_parts = jnp.einsum("rnd,ndf->rnf", gathered, up_blocks)
        gate_sum = jnp.sum(gate_parts, axis=1)
        up_sum = jnp.sum(up_parts, axis=1)
        hidden = (jax.nn.silu(gate_sum) * up_sum).astype(jnp.bfloat16)
        expert_out = jnp.dot(hidden, down_weight[expert], preferred_element_type=jnp.float32).astype(jnp.bfloat16)
        picked = expert_out[jnp.where(chosen, slot_of, 0).astype(jnp.int32)]
        return carry + weight_of[:, None] * picked.astype(jnp.float32), None

    start = jnp.zeros((total, features), jnp.float32)
    mixed, _ = lax.scan(one_expert, start, jnp.arange(experts, dtype=jnp.int32))
    return mixed.astype(jnp.bfloat16)
```

```python
import functools

import jax
import jax.numpy as jnp
from jax import lax
from jax.experimental import pallas as pl
from jax.experimental.pallas import tpu as pltpu
from jax.sharding import PartitionSpec as P

SLOTS = 48
HALF = 24
STRIP = 256

VMEM = pl.BlockSpec(memory_space=pltpu.VMEM)
SMEM = pl.BlockSpec(memory_space=pltpu.SMEM)
NT = (((1,), (1,)), ((), ()))
LIMIT = pltpu.CompilerParams(vmem_limit_bytes=40 * 1024 * 1024)


def column(row, experts):
    first = lax.broadcasted_iota(jnp.int32, (experts, experts), 0)
    second = lax.broadcasted_iota(jnp.int32, (experts, experts), 1)
    spread = jnp.where(first == second, jnp.broadcast_to(row, (experts, experts)), 0.0)
    return jnp.sum(spread, axis=1, keepdims=True)


def ranks(routes, capacity, spill):
    experts = capacity.shape[1]
    top, tokens = routes.shape
    number = lax.broadcasted_iota(jnp.int32, (experts, tokens), 0)
    named = jnp.zeros((experts, tokens), jnp.float32)
    for k in range(top):
        named = named + jnp.where(routes[k : k + 1, :] == number, 1.0, 0.0)
    earlier = lax.broadcasted_iota(jnp.int32, (tokens, tokens), 0) < lax.broadcasted_iota(
        jnp.int32, (tokens, tokens), 1
    )
    before = jnp.dot(
        named.astype(jnp.bfloat16),
        jnp.where(earlier, 1.0, 0.0).astype(jnp.bfloat16),
        preferred_element_type=jnp.float32,
    )
    limit = column((capacity + spill).astype(jnp.float32), experts)
    return jnp.where((named > 0.0) & (before < limit), before, -1.0)


def pick_kernel(core, routes, capacity, spill, tokens, tokens_other, rows):
    rank = ranks(routes[...], capacity[...], spill[...])
    experts, count = rank.shape
    slot = lax.broadcasted_iota(jnp.int32, (experts, HALF, count), 1) + core[0] * HALF
    pick = jnp.where(rank[:, None, :] == slot.astype(jnp.float32), 1.0, 0.0)
    pick = pick.reshape(experts * HALF, count).astype(jnp.bfloat16)
    features = jnp.concatenate([tokens[...], tokens_other[...]], axis=0)
    picked = lax.dot_general(pick, features, NT, preferred_element_type=jnp.float32)
    rows[...] = picked.astype(jnp.bfloat16)


def weigh_kernel(routes, weights, capacity, spill, weigh):
    rank = ranks(routes[...], capacity[...], spill[...])
    experts, count = rank.shape
    value = weights[...].astype(jnp.float32)
    share = value / jnp.sum(value, axis=0, keepdims=True)
    number = lax.broadcasted_iota(jnp.int32, (experts, count), 0)
    share_of = jnp.zeros((experts, count), jnp.float32)
    for k in range(value.shape[0]):
        share_of = share_of + jnp.where(routes[k : k + 1, :] == number, share[k : k + 1, :], 0.0)
    slot = lax.broadcasted_iota(jnp.int32, (experts, SLOTS, count), 1).astype(jnp.float32)
    table = jnp.where(rank[:, None, :] == slot, share_of[:, None, :], 0.0)
    table = table.reshape(experts * SLOTS, count).T
    upper = table.astype(jnp.bfloat16)
    lower = (table - upper.astype(jnp.float32)).astype(jnp.bfloat16)
    weigh[0:count, :] = upper
    weigh[count : 2 * count, :] = lower


def project_kernel(rows, gate, gate_other, up, up_other, sums):
    for at, (own, other) in enumerate(((gate, gate_other), (up, up_other))):
        weight = jnp.concatenate([own[...], other[...]], axis=0)
        part = jnp.dot(rows[...], weight, preferred_element_type=jnp.float32)
        sums[:, at * STRIP : (at + 1) * STRIP] = part.astype(jnp.bfloat16)


def hidden_kernel(sums, hidden):
    for strip in range(hidden.shape[1] // STRIP):
        at = 2 * STRIP * strip
        gate = sums[:, at : at + STRIP].astype(jnp.float32)
        up = sums[:, at + STRIP : at + 2 * STRIP].astype(jnp.float32)
        value = gate / (1.0 + jnp.exp(-gate)) * up
        hidden[:, STRIP * strip : STRIP * (strip + 1)] = value.astype(jnp.bfloat16)


def down_kernel(hidden, down, out):
    pairs, _, depth, width = hidden.shape
    for pair in range(pairs):
        both = hidden[pair].reshape(2 * depth, width)
        value = lax.dot_general(both, down[...], NT, preferred_element_type=jnp.float32)
        for j in range(depth // HALF):
            first = value[j * HALF : (j + 1) * HALF]
            second = value[depth + j * HALF : depth + (j + 1) * HALF]
            block = jnp.concatenate([first, second], axis=0)
            out[pair * (depth // HALF) + j] = block.astype(jnp.bfloat16)


def mix_kernel(weigh, values, mixed):
    total = jnp.dot(weigh[...], values[...], preferred_element_type=jnp.float32)
    count = total.shape[0] // 2
    mixed[...] = (total[:count] + total[count:]).T.astype(jnp.bfloat16)


def cost(flops, moved):
    return pl.CostEstimate(flops=flops, bytes_accessed=moved, transcendentals=0)


def on_device(
    tokens, routes, weights_int, capacity, spill_size, gate_weight, up_weight, down_weight
):
    experts = capacity.shape[0]
    groups = lax.axis_size("ep")
    planes = lax.axis_size("dp") // 2
    count, features = tokens.shape
    units = gate_weight.shape[2]
    bf16 = jnp.bfloat16
    core = (lax.axis_index("dp") % 2).astype(jnp.int32).reshape(1)
    swap = [(i, i ^ 1) for i in range(2 * planes)]
    same_core = [[2 * z + c for z in range(planes)] for c in range(2)]

    own_tokens = tokens.T
    own_routes = routes.T
    own_weights = weights_int.T
    cap_row = capacity.reshape(1, experts)
    spill_row = spill_size.reshape(1, experts)
    gate = gate_weight[0]
    up = up_weight[0]
    down = down_weight[0].T

    tokens_other = lax.ppermute(own_tokens, "dp", swap)
    gate_other = lax.ppermute(gate, "dp", swap)
    up_other = lax.ppermute(up, "dp", swap)

    send = pl.pallas_call(
        pick_kernel,
        out_shape=jax.ShapeDtypeStruct((experts * HALF, 2 * features), bf16),
        in_specs=[SMEM] + [VMEM] * 5,
        out_specs=VMEM,
        compiler_params=LIMIT,
        cost_estimate=cost(2 * experts * HALF * count * 2 * features, 2000000),
        name="pick_rows",
    )(core, own_routes, cap_row, spill_row, own_tokens, tokens_other)
    got = lax.all_to_all(
        send.reshape(groups, HALF, 2 * features), "ep", split_axis=0, concat_axis=0, tiled=True
    ).reshape(groups * HALF, 2 * features)

    depth = groups * HALF
    wide = pl.BlockSpec((features, STRIP), lambda i: (0, i))
    sums = pl.pallas_call(
        project_kernel,
        grid=(units // STRIP,),
        out_shape=jax.ShapeDtypeStruct((depth, 2 * units), bf16),
        in_specs=[pl.BlockSpec((depth, 2 * features), lambda i: (0, 0))] + [wide] * 4,
        out_specs=pl.BlockSpec((depth, 2 * STRIP), lambda i: (0, i)),
        compiler_params=LIMIT,
        cost_estimate=cost(2 * depth * 2 * features * 2 * units, 8000000),
        name="project_in",
    )(got, gate, gate_other, up, up_other)
    summed = lax.psum_scatter(
        sums, "dp", scatter_dimension=0, tiled=True, axis_index_groups=same_core
    )
    weigh = pl.pallas_call(
        weigh_kernel,
        out_shape=jax.ShapeDtypeStruct((2 * count, experts * SLOTS), bf16),
        in_specs=[VMEM] * 4,
        out_specs=VMEM,
        compiler_params=LIMIT,
        cost_estimate=cost(2 * experts * count * count, 4000000),
        name="weigh_table",
    )(own_routes, own_weights, cap_row, spill_row)
    part = depth // planes
    hidden = pl.pallas_call(
        hidden_kernel,
        out_shape=jax.ShapeDtypeStruct((part, units), bf16),
        in_specs=[VMEM],
        out_specs=VMEM,
        compiler_params=LIMIT,
        cost_estimate=cost(8 * part * units, 600000),
        name="hidden_units",
    )(summed)
    all_hidden = lax.all_gather(hidden, "dp", axis=0, tiled=True)
    all_hidden = all_hidden.reshape(planes, 2, part, units)

    at_once = 2
    blocks = at_once * part // HALF
    back = pl.pallas_call(
        down_kernel,
        grid=(planes // at_once,),
        out_shape=jax.ShapeDtypeStruct((groups, SLOTS, features), bf16),
        in_specs=[
            pl.BlockSpec((at_once, 2, part, units), lambda i: (i, 0, 0, 0)),
            pl.BlockSpec((features, units), lambda i: (0, 0)),
        ],
        out_specs=pl.BlockSpec((blocks, SLOTS, features), lambda i: (i, 0, 0)),
        compiler_params=LIMIT,
        cost_estimate=cost(2 * 2 * depth * units * features, 6000000),
        name="project_out",
    )(all_hidden, down)
    values = lax.all_to_all(back, "ep", split_axis=0, concat_axis=0, tiled=True)
    mixed = pl.pallas_call(
        mix_kernel,
        out_shape=jax.ShapeDtypeStruct((features, count), bf16),
        in_specs=[VMEM] * 2,
        out_specs=VMEM,
        compiler_params=LIMIT,
        cost_estimate=cost(4 * count * experts * SLOTS * features, 3000000),
        name="mix_rows",
    )(weigh, values.reshape(experts * SLOTS, features))
    return mixed.T


def solution(mesh):
    placed = (
        P("ep", "dp"),
        P("ep", None),
        P("ep", None),
        P(),
        P(),
        P("ep", "dp", None),
        P("ep", "dp", None),
        P("ep", None, "dp"),
    )
    return jax.shard_map(
        on_device, mesh=mesh, in_specs=placed, out_specs=P("ep", "dp"), check_vma=False
    )
```

```python
import functools

import jax
import jax.numpy as jnp
from jax import lax
from jax.experimental import pallas as pl
from jax.experimental.pallas import tpu as pltpu
from jax.sharding import PartitionSpec as P

HALF = 24
STRIP = 256

VMEM = pl.BlockSpec(memory_space=pltpu.VMEM)
SMEM = pl.BlockSpec(memory_space=pltpu.SMEM)
NT = (((1,), (1,)), ((), ()))
LIMIT = pltpu.CompilerParams(vmem_limit_bytes=60 * 1024 * 1024)


def column(row, experts):
    first = lax.broadcasted_iota(jnp.int32, (experts, experts), 0)
    second = lax.broadcasted_iota(jnp.int32, (experts, experts), 1)
    spread = jnp.where(first == second, jnp.broadcast_to(row, (experts, experts)), 0.0)
    return jnp.sum(spread, axis=1, keepdims=True)


def ranks(routes, capacity, spill):
    experts = capacity.shape[1]
    top, tokens = routes.shape
    number = lax.broadcasted_iota(jnp.int32, (experts, tokens), 0)
    named = jnp.zeros((experts, tokens), jnp.float32)
    for k in range(top):
        named = named + jnp.where(routes[k : k + 1, :] == number, 1.0, 0.0)
    earlier = lax.broadcasted_iota(jnp.int32, (tokens, tokens), 0) < lax.broadcasted_iota(
        jnp.int32, (tokens, tokens), 1
    )
    before = jnp.dot(
        named.astype(jnp.bfloat16),
        jnp.where(earlier, 1.0, 0.0).astype(jnp.bfloat16),
        preferred_element_type=jnp.float32,
    )
    limit = column((capacity + spill).astype(jnp.float32), experts)
    return jnp.where((named > 0.0) & (before < limit), before, -1.0)


def pick_kernel(core, routes, capacity, spill, tokens, tokens_other, rows):
    rank = ranks(routes[...], capacity[...], spill[...])
    experts, count = rank.shape
    slot = lax.broadcasted_iota(jnp.int32, (experts, HALF, count), 1) + core[0] * HALF
    pick = jnp.where(rank[:, None, :] == slot.astype(jnp.float32), 1.0, 0.0)
    pick = pick.reshape(experts * HALF, count).astype(jnp.bfloat16)
    features = jnp.concatenate([tokens[...], tokens_other[...]], axis=0)
    picked = lax.dot_general(pick, features, NT, preferred_element_type=jnp.float32)
    rows[...] = picked.astype(jnp.bfloat16)


def weigh_kernel(routes, weights, capacity, spill, weigh):
    rank = ranks(routes[...], capacity[...], spill[...])
    experts, count = rank.shape
    value = weights[...].astype(jnp.float32)
    share = value / jnp.sum(value, axis=0, keepdims=True)
    number = lax.broadcasted_iota(jnp.int32, (experts, count), 0)
    share_of = jnp.zeros((experts, count), jnp.float32)
    for k in range(value.shape[0]):
        share_of = share_of + jnp.where(routes[k : k + 1, :] == number, share[k : k + 1, :], 0.0)
    slot = lax.broadcasted_iota(jnp.int32, (experts, HALF, count), 1).astype(jnp.float32)
    for half in range(2):
        table = jnp.where(rank[:, None, :] == slot + half * HALF, share_of[:, None, :], 0.0)
        table = table.reshape(experts * HALF, count).T
        upper = table.astype(jnp.bfloat16)
        lower = (table - upper.astype(jnp.float32)).astype(jnp.bfloat16)
        weigh[half, 0:count, :] = upper
        weigh[half, count : 2 * count, :] = lower


def project_kernel(rows, gate, gate_other, up, up_other, sums):
    for at, (own, other) in enumerate(((gate, gate_other), (up, up_other))):
        weight = jnp.concatenate([own[...], other[...]], axis=0)
        part = jnp.dot(rows[...], weight, preferred_element_type=jnp.float32)
        sums[:, at * STRIP : (at + 1) * STRIP] = part.astype(jnp.bfloat16)


def hidden_kernel(sums, hidden):
    for strip in range(hidden.shape[1] // STRIP):
        at = 2 * STRIP * strip
        gate = sums[:, at : at + STRIP].astype(jnp.float32)
        up = sums[:, at + STRIP : at + 2 * STRIP].astype(jnp.float32)
        value = gate / (1.0 + jnp.exp(-gate)) * up
        hidden[:, STRIP * strip : STRIP * (strip + 1)] = value.astype(jnp.bfloat16)


def down_kernel(hidden, down, out):
    pairs, _, depth, width = hidden.shape
    features = down.shape[0]
    for half in range(2):
        rows = hidden[:, half].reshape(pairs * depth, width)
        value = lax.dot_general(rows, down[...], NT, preferred_element_type=jnp.float32)
        out[:, half * features : (half + 1) * features] = value.astype(jnp.bfloat16)


def mix_kernel(weigh, values, mixed):
    features, count = mixed.shape
    total = jnp.zeros((features, count), jnp.float32)
    for half in range(2):
        part = jnp.dot(weigh[half], values[...], preferred_element_type=jnp.float32)
        part = (part[:count] + part[count:]).T
        total = total + part[half * features : (half + 1) * features]
    mixed[...] = total.astype(jnp.bfloat16)


def cost(flops, moved):
    return pl.CostEstimate(flops=flops, bytes_accessed=moved, transcendentals=0)


def on_device(
    tokens, routes, weights_int, capacity, spill_size, gate_weight, up_weight, down_weight
):
    experts = capacity.shape[0]
    groups = lax.axis_size("ep")
    planes = lax.axis_size("dp") // 2
    count, features = tokens.shape
    units = gate_weight.shape[2]
    bf16 = jnp.bfloat16
    core = (lax.axis_index("dp") % 2).astype(jnp.int32).reshape(1)
    swap = [(i, i ^ 1) for i in range(2 * planes)]
    same_core = [[2 * z + c for z in range(planes)] for c in range(2)]

    own_tokens = tokens.T
    own_routes = routes.T
    own_weights = weights_int.T
    cap_row = capacity.reshape(1, experts)
    spill_row = spill_size.reshape(1, experts)
    gate = gate_weight[0]
    up = up_weight[0]
    down = down_weight[0].T

    tokens_other = lax.ppermute(own_tokens, "dp", swap)
    gate_other = lax.ppermute(gate, "dp", swap)
    up_other = lax.ppermute(up, "dp", swap)

    send = pl.pallas_call(
        pick_kernel,
        out_shape=jax.ShapeDtypeStruct((experts * HALF, 2 * features), bf16),
        in_specs=[SMEM] + [VMEM] * 5,
        out_specs=VMEM,
        compiler_params=LIMIT,
        cost_estimate=cost(2 * experts * HALF * count * 2 * features, 2000000),
        name="pick_rows",
    )(core, own_routes, cap_row, spill_row, own_tokens, tokens_other)
    got = lax.all_to_all(
        send.reshape(groups, HALF, 2 * features), "ep", split_axis=0, concat_axis=0, tiled=True
    ).reshape(groups * HALF, 2 * features)

    depth = groups * HALF
    wide = pl.BlockSpec((features, STRIP), lambda i: (0, i))
    sums = pl.pallas_call(
        project_kernel,
        grid=(units // STRIP,),
        out_shape=jax.ShapeDtypeStruct((depth, 2 * units), bf16),
        in_specs=[pl.BlockSpec((depth, 2 * features), lambda i: (0, 0))] + [wide] * 4,
        out_specs=pl.BlockSpec((depth, 2 * STRIP), lambda i: (0, i)),
        compiler_params=LIMIT,
        cost_estimate=cost(2 * depth * 2 * features * 2 * units, 8000000),
        name="project_in",
    )(got, gate, gate_other, up, up_other)
    summed = lax.psum_scatter(
        sums, "dp", scatter_dimension=0, tiled=True, axis_index_groups=same_core
    )
    weigh = pl.pallas_call(
        weigh_kernel,
        out_shape=jax.ShapeDtypeStruct((2, 2 * count, experts * HALF), bf16),
        in_specs=[VMEM] * 4,
        out_specs=VMEM,
        compiler_params=LIMIT,
        cost_estimate=cost(2 * experts * count * count, 4000000),
        name="weigh_table",
    )(own_routes, own_weights, cap_row, spill_row)
    part = depth // planes
    hidden = pl.pallas_call(
        hidden_kernel,
        out_shape=jax.ShapeDtypeStruct((part, units), bf16),
        in_specs=[VMEM],
        out_specs=VMEM,
        compiler_params=LIMIT,
        cost_estimate=cost(8 * part * units, 600000),
        name="hidden_units",
    )(summed)
    all_hidden = lax.all_gather(hidden, "dp", axis=0, tiled=True)
    all_hidden = all_hidden.reshape(planes, 2, part, units)

    at_once = 2
    back = pl.pallas_call(
        down_kernel,
        grid=(planes // at_once,),
        out_shape=jax.ShapeDtypeStruct((depth, 2 * features), bf16),
        in_specs=[
            pl.BlockSpec((at_once, 2, part, units), lambda i: (i, 0, 0, 0)),
            pl.BlockSpec((features, units), lambda i: (0, 0)),
        ],
        out_specs=pl.BlockSpec((at_once * part, 2 * features), lambda i: (i, 0)),
        compiler_params=LIMIT,
        cost_estimate=cost(2 * 2 * depth * units * features, 6000000),
        name="project_out",
    )(all_hidden, down)
    back = back.reshape(groups, HALF, 2 * features)
    values = lax.all_to_all(back, "ep", split_axis=0, concat_axis=0, tiled=True)
    mixed = pl.pallas_call(
        mix_kernel,
        out_shape=jax.ShapeDtypeStruct((features, count), bf16),
        in_specs=[VMEM] * 2,
        out_specs=VMEM,
        compiler_params=LIMIT,
        cost_estimate=cost(8 * count * experts * HALF * 2 * features, 3000000),
        name="mix_rows",
    )(weigh, values.reshape(experts * HALF, 2 * features))
    return mixed.T


def solution(mesh):
    placed = (
        P("ep", "dp"),
        P("ep", None),
        P("ep", None),
        P(),
        P(),
        P("ep", "dp", None),
        P("ep", "dp", None),
        P("ep", None, "dp"),
    )
    return jax.shard_map(
        on_device, mesh=mesh, in_specs=placed, out_specs=P("ep", "dp"), check_vma=False
    )
```

```python
import jax
import jax.numpy as jnp
from jax import lax
from jax.experimental import pallas as pl
from jax.experimental.pallas import tpu as pltpu
from jax.sharding import PartitionSpec as P

HALF = 24
PIECES = 4
STRIP = 256

VMEM = pl.BlockSpec(memory_space=pltpu.VMEM)
SMEM = pl.BlockSpec(memory_space=pltpu.SMEM)
NT = (((1,), (1,)), ((), ()))
HBM = pl.BlockSpec(memory_space=pltpu.HBM)
LIMIT = pltpu.CompilerParams(vmem_limit_bytes=40 * 1024 * 1024)
LARGE = pltpu.CompilerParams(vmem_limit_bytes=60 * 1024 * 1024)


def column(row, experts):
    first = lax.broadcasted_iota(jnp.int32, (experts, experts), 0)
    second = lax.broadcasted_iota(jnp.int32, (experts, experts), 1)
    spread = jnp.where(first == second, jnp.broadcast_to(row, (experts, experts)), 0.0)
    return jnp.sum(spread, axis=1, keepdims=True)


def ranks(routes, capacity, spill):
    experts = capacity.shape[1]
    top, tokens = routes.shape
    number = lax.broadcasted_iota(jnp.int32, (experts, tokens), 0)
    named = jnp.zeros((experts, tokens), jnp.float32)
    for k in range(top):
        named = named + jnp.where(routes[k : k + 1, :] == number, 1.0, 0.0)
    earlier = lax.broadcasted_iota(jnp.int32, (tokens, tokens), 0) < lax.broadcasted_iota(
        jnp.int32, (tokens, tokens), 1
    )
    before = jnp.dot(
        named.astype(jnp.bfloat16),
        jnp.where(earlier, 1.0, 0.0).astype(jnp.bfloat16),
        preferred_element_type=jnp.float32,
    )
    limit = column((capacity + spill).astype(jnp.float32), experts)
    return jnp.where((named > 0.0) & (before < limit), before, -1.0)


def table_kernel(core, routes, capacity, spill, tokens, pick, kept, named, limits, sem):
    copies = [
        pltpu.make_async_copy(routes, named, sem.at[0]),
        pltpu.make_async_copy(capacity, limits.at[0:1], sem.at[1]),
        pltpu.make_async_copy(spill, limits.at[1:2], sem.at[2]),
        pltpu.make_async_copy(tokens, kept, sem.at[3]),
    ]
    for copy in copies:
        copy.start()
    for copy in copies[:3]:
        copy.wait()
    rank = ranks(named[...], limits[0:1, :], limits[1:2, :])
    experts, count = rank.shape
    slot = lax.broadcasted_iota(jnp.int32, (experts, HALF, count), 1) + core[0] * HALF
    chosen = jnp.where(rank[:, None, :] == slot.astype(jnp.float32), 1.0, 0.0)
    pick[...] = chosen.reshape(experts * HALF, count).astype(jnp.bfloat16)
    copies[3].wait()


def pick_kernel(pick, tokens, tokens_other, rows, held, sem):
    features = jnp.concatenate([tokens[...], tokens_other[...]], axis=0)
    piece = rows.shape[0] // PIECES
    copies = []
    for k in range(PIECES):
        at = pl.ds(k * piece, piece)
        picked = lax.dot_general(pick[at, :], features, NT, preferred_element_type=jnp.float32)
        held[at, :] = picked.astype(jnp.bfloat16)
        copies.append(pltpu.make_async_copy(held.at[at], rows.at[at], sem.at[k]))
        copies[-1].start()
    for copy in copies:
        copy.wait()


def weigh_kernel(routes, weights, capacity, spill, weigh):
    rank = ranks(routes[...], capacity[...], spill[...])
    experts, count = rank.shape
    value = weights[...].astype(jnp.float32)
    share = value / jnp.sum(value, axis=0, keepdims=True)
    number = lax.broadcasted_iota(jnp.int32, (experts, count), 0)
    share_of = jnp.zeros((experts, count), jnp.float32)
    for k in range(value.shape[0]):
        share_of = share_of + jnp.where(routes[k : k + 1, :] == number, share[k : k + 1, :], 0.0)
    slot = lax.broadcasted_iota(jnp.int32, (experts, HALF, count), 1).astype(jnp.float32)
    for half in range(2):
        table = jnp.where(rank[:, None, :] == slot + half * HALF, share_of[:, None, :], 0.0)
        table = table.reshape(experts * HALF, count).T
        upper = table.astype(jnp.bfloat16)
        lower = (table - upper.astype(jnp.float32)).astype(jnp.bfloat16)
        weigh[half, 0:count, :] = upper
        weigh[half, count : 2 * count, :] = lower


def project_kernel(rows, gate, gate_other, up, up_other, sums, held, weight, result, came, went):
    depth, width = held.shape
    features = width // 2
    strips = gate.shape[1] // STRIP
    piece = depth // PIECES
    loads = []
    for k in range(PIECES):
        at = pl.ds(k * piece, piece)
        loads.append(pltpu.make_async_copy(rows.at[at], held.at[at], came.at[k]))
        loads[-1].start()
    sources = ((gate, 0, 0), (gate_other, 1, 0), (up, 0, 1), (up_other, 1, 1))
    fetched = []
    for strip in range(strips):
        for n, (source, low, kind) in enumerate(sources):
            copy = pltpu.make_async_copy(
                source.at[:, pl.ds(strip * STRIP, STRIP)],
                weight.at[strip, kind, pl.ds(low * features, features)],
                came.at[PIECES + strip * len(sources) + n],
            )
            copy.start()
            fetched.append(copy)
    for copy in loads:
        copy.wait()
    stores = []
    for strip in range(strips):
        for copy in fetched[strip * len(sources) : (strip + 1) * len(sources)]:
            copy.wait()
        for kind in range(2):
            part = jnp.dot(held[...], weight[strip, kind], preferred_element_type=jnp.float32)
            result[strip, :, kind * STRIP : (kind + 1) * STRIP] = part.astype(jnp.bfloat16)
        for k in range(PIECES):
            at = pl.ds(k * piece, piece)
            copy = pltpu.make_async_copy(
                result.at[strip, at],
                sums.at[at, pl.ds(strip * 2 * STRIP, 2 * STRIP)],
                went.at[strip * PIECES + k],
            )
            copy.start()
            stores.append(copy)
    for copy in stores:
        copy.wait()


def hidden_kernel(sums, hidden):
    for strip in range(hidden.shape[1] // STRIP):
        at = 2 * STRIP * strip
        gate = sums[:, at : at + STRIP].astype(jnp.float32)
        up = sums[:, at + STRIP : at + 2 * STRIP].astype(jnp.float32)
        value = gate / (1.0 + jnp.exp(-gate)) * up
        hidden[:, STRIP * strip : STRIP * (strip + 1)] = value.astype(jnp.bfloat16)


def down_kernel(places, parts, down, out, held, sem, first):
    depth = held.shape[1]
    features = down.shape[0]
    copies = []
    for part, chips in parts:
        value = lax.dot_general(part, down[...], NT, preferred_element_type=jnp.float32)
        value = value.astype(jnp.bfloat16)
        for n, chip in enumerate(chips):
            low = value[2 * n * depth : (2 * n + 1) * depth]
            high = value[(2 * n + 1) * depth : (2 * n + 2) * depth]
            swapped = places[1, chip] == 1
            slot = chip - first
            held[slot, :, 0:features] = jnp.where(swapped, high, low)
            held[slot, :, features : 2 * features] = jnp.where(swapped, low, high)
            place = pl.multiple_of(places[0, chip] * depth, depth)
            copies.append(
                pltpu.make_async_copy(held.at[slot], out.at[pl.ds(place, depth)], sem.at[slot])
            )
            copies[-1].start()
    for copy in copies:
        copy.wait()


def early_kernel(places, own, near, far, swapped_pair, down, out, held, sem):
    rows = jnp.concatenate([own[...], near[...], far[...]], axis=0)
    parts = ((rows, (0, 1, 2)), (swapped_pair[...], (3, 4)))
    down_kernel(places, parts, down, out, held, sem, 0)


def late_kernel(places, third, fourth, swapped, down, filled, out, held, sem):
    del filled
    depth = fourth.shape[0]
    rows = jnp.concatenate([third[...], swapped[0 : 2 * depth]], axis=0)
    last = jnp.concatenate([fourth[...], swapped[2 * depth : 3 * depth]], axis=0)
    parts = ((rows, (5, 6)), (last, (7,)))
    down_kernel(places, parts, down, out, held, sem, 5)


def mix_kernel(weigh, values, mixed):
    features, count = mixed.shape
    total = jnp.zeros((features, count), jnp.float32)
    for half in range(2):
        part = jnp.dot(weigh[half], values[...], preferred_element_type=jnp.float32)
        part = (part[:count] + part[count:]).T
        total = total + part[half * features : (half + 1) * features]
    mixed[...] = total.astype(jnp.bfloat16)


def cost(flops, moved):
    return pl.CostEstimate(flops=flops, bytes_accessed=moved, transcendentals=0)


def on_device(
    tokens, routes, weights_int, capacity, spill_size, gate_weight, up_weight, down_weight
):
    experts = capacity.shape[0]
    groups = lax.axis_size("ep")
    planes = lax.axis_size("dp") // 2
    count, features = tokens.shape
    units = gate_weight.shape[2]
    bf16 = jnp.bfloat16
    core = (lax.axis_index("dp") % 2).astype(jnp.int32).reshape(1)
    swap = [(i, i ^ 1) for i in range(2 * planes)]
    same_core = [[2 * z + c for z in range(planes)] for c in range(2)]

    own_tokens = tokens.T
    own_routes = routes.T
    own_weights = weights_int.T
    cap_row = capacity.reshape(1, experts)
    spill_row = spill_size.reshape(1, experts)
    gate = gate_weight[0]
    up = up_weight[0]
    down = down_weight[0].T

    tokens_other = lax.ppermute(own_tokens, "dp", swap)
    gate_other = lax.ppermute(gate, "dp", swap)
    up_other = lax.ppermute(up, "dp", swap)

    pick, kept_tokens = pl.pallas_call(
        table_kernel,
        out_shape=[
            jax.ShapeDtypeStruct((experts * HALF, count), bf16),
            jax.ShapeDtypeStruct((features, count), bf16),
        ],
        in_specs=[SMEM] + [HBM] * 4,
        out_specs=[VMEM] * 2,
        scratch_shapes=[
            pltpu.VMEM(own_routes.shape, jnp.int32),
            pltpu.VMEM((2, experts), jnp.int32),
            pltpu.SemaphoreType.DMA((4,)),
        ],
        compiler_params=LIMIT,
        cost_estimate=cost(2 * experts * count * count, 600000),
        name="pick_table",
    )(core, own_routes, cap_row, spill_row, own_tokens)
    send = pl.pallas_call(
        pick_kernel,
        out_shape=jax.ShapeDtypeStruct((experts * HALF, 2 * features), bf16),
        in_specs=[VMEM] * 3,
        out_specs=HBM,
        scratch_shapes=[
            pltpu.VMEM((experts * HALF, 2 * features), bf16),
            pltpu.SemaphoreType.DMA((PIECES,)),
        ],
        compiler_params=LIMIT,
        cost_estimate=cost(2 * experts * HALF * count * 2 * features, 2000000),
        name="pick_rows",
    )(pick, kept_tokens, tokens_other)
    got = lax.all_to_all(
        send.reshape(groups, HALF, 2 * features), "ep", split_axis=0, concat_axis=0, tiled=True
    ).reshape(groups * HALF, 2 * features)

    depth = groups * HALF
    strips = units // STRIP
    sums = pl.pallas_call(
        project_kernel,
        out_shape=jax.ShapeDtypeStruct((depth, 2 * units), bf16),
        in_specs=[HBM] * 5,
        out_specs=HBM,
        scratch_shapes=[
            pltpu.VMEM((depth, 2 * features), bf16),
            pltpu.VMEM((strips, 2, 2 * features, STRIP), bf16),
            pltpu.VMEM((strips, depth, 2 * STRIP), bf16),
            pltpu.SemaphoreType.DMA((PIECES + 4 * strips,)),
            pltpu.SemaphoreType.DMA((strips * PIECES,)),
        ],
        compiler_params=LARGE,
        cost_estimate=cost(2 * depth * 2 * features * 2 * units, 8000000),
        name="project_in",
    )(got, gate, gate_other, up, up_other)
    summed = lax.psum_scatter(
        sums, "dp", scatter_dimension=0, tiled=True, axis_index_groups=same_core
    )
    weigh = pl.pallas_call(
        weigh_kernel,
        out_shape=jax.ShapeDtypeStruct((2, 2 * count, experts * HALF), bf16),
        in_specs=[VMEM] * 4,
        out_specs=VMEM,
        compiler_params=LIMIT,
        cost_estimate=cost(2 * experts * count * count, 4000000),
        name="weigh_table",
    )(own_routes, own_weights, cap_row, spill_row)
    part = depth // planes
    hidden = pl.pallas_call(
        hidden_kernel,
        out_shape=jax.ShapeDtypeStruct((part, units), bf16),
        in_specs=[VMEM],
        out_specs=VMEM,
        compiler_params=LIMIT,
        cost_estimate=cost(8 * part * units, 600000),
        name="hidden_units",
    )(summed)

    def flow(rows, hops):
        steps = [
            (2 * z + c, 2 * ((z + (hops, -hops)[c]) % planes) + c)
            for z in range(planes)
            for c in range(2)
        ]
        return lax.ppermute(rows, "dp", steps)

    own = jnp.concatenate([hidden, lax.ppermute(hidden, "dp", swap)], axis=0)
    near, far = flow(own, 1), flow(own, 2)
    third, fourth = flow(far, 1), flow(far[:part], 2)
    swapped_pair = lax.ppermute(jnp.concatenate([near, far], axis=0), "dp", swap)
    swapped_last = lax.ppermute(jnp.concatenate([third, fourth], axis=0), "dp", swap)
    plane = lax.axis_index("dp") // 2
    sense = 2 * core[0] - 1
    chips = [0, sense, 2 * sense, -sense, -2 * sense, 3 * sense, -3 * sense, 4]
    orders = [core[0]] * 3 + [1 - core[0]] * 2 + [core[0], 1 - core[0], core[0]]
    places = jnp.stack(
        [jnp.stack([(plane + chip + planes) % planes for chip in chips]), jnp.stack(orders)]
    ).astype(jnp.int32)
    back_shape = jax.ShapeDtypeStruct((depth, 2 * features), bf16)

    def scratch(held):
        return [
            pltpu.VMEM((held, part, 2 * features), bf16),
            pltpu.SemaphoreType.DMA((held,)),
        ]

    back = pl.pallas_call(
        early_kernel,
        out_shape=back_shape,
        in_specs=[SMEM] + [VMEM] * 5,
        out_specs=HBM,
        scratch_shapes=scratch(5),
        compiler_params=LIMIT,
        cost_estimate=cost(20 * part * units * features, 4000000),
        name="project_out_early",
    )(places, own, near, far, swapped_pair, down)
    back = pl.pallas_call(
        late_kernel,
        out_shape=back_shape,
        in_specs=[SMEM] + [VMEM] * 4 + [HBM],
        out_specs=HBM,
        scratch_shapes=scratch(3),
        input_output_aliases={5: 0},
        compiler_params=LIMIT,
        cost_estimate=cost(12 * part * units * features, 4000000),
        name="project_out_late",
    )(places, third, fourth, swapped_last, down, back)
    back = back.reshape(groups, HALF, 2 * features)
    values = lax.all_to_all(back, "ep", split_axis=0, concat_axis=0, tiled=True)
    mixed = pl.pallas_call(
        mix_kernel,
        out_shape=jax.ShapeDtypeStruct((features, count), bf16),
        in_specs=[VMEM] * 2,
        out_specs=VMEM,
        compiler_params=LIMIT,
        cost_estimate=cost(8 * count * experts * HALF * 2 * features, 3000000),
        name="mix_rows",
    )(weigh, values.reshape(experts * HALF, 2 * features))
    return mixed.T


def solution(mesh):
    placed = (
        P("ep", "dp"),
        P("ep", None),
        P("ep", None),
        P(),
        P(),
        P("ep", "dp", None),
        P("ep", "dp", None),
        P("ep", None, "dp"),
    )
    return jax.shard_map(
        on_device, mesh=mesh, in_specs=placed, out_specs=P("ep", "dp"), check_vma=False
    )
```

```python
import functools

import jax
import jax.numpy as jnp
from jax import lax
from jax.experimental import pallas as pl
from jax.experimental.pallas import tpu as pltpu
from jax.sharding import PartitionSpec as P

HALF = 24
ROOM = 77824
HELD = 20
PIECES = 4
STRIP = 256

VMEM = pl.BlockSpec(memory_space=pltpu.VMEM)
SMEM = pl.BlockSpec(memory_space=pltpu.SMEM)
NT = (((1,), (1,)), ((), ()))
HBM = pl.BlockSpec(memory_space=pltpu.HBM)
LIMIT = pltpu.CompilerParams(vmem_limit_bytes=40 * 1024 * 1024)
LARGE = pltpu.CompilerParams(vmem_limit_bytes=60 * 1024 * 1024)


def column(row, experts):
    first = lax.broadcasted_iota(jnp.int32, (experts, experts), 0)
    second = lax.broadcasted_iota(jnp.int32, (experts, experts), 1)
    spread = jnp.where(first == second, jnp.broadcast_to(row, (experts, experts)), 0.0)
    return jnp.sum(spread, axis=1, keepdims=True)


def ranks(routes, capacity, spill):
    experts = capacity.shape[1]
    top, tokens = routes.shape
    number = lax.broadcasted_iota(jnp.int32, (experts, tokens), 0)
    named = jnp.zeros((experts, tokens), jnp.float32)
    for k in range(top):
        named = named + jnp.where(routes[k : k + 1, :] == number, 1.0, 0.0)
    earlier = lax.broadcasted_iota(jnp.int32, (tokens, tokens), 0) < lax.broadcasted_iota(
        jnp.int32, (tokens, tokens), 1
    )
    before = jnp.dot(
        named.astype(jnp.bfloat16),
        jnp.where(earlier, 1.0, 0.0).astype(jnp.bfloat16),
        preferred_element_type=jnp.float32,
    )
    limit = column((capacity + spill).astype(jnp.float32), experts)
    return jnp.where((named > 0.0) & (before < limit), before, -1.0)


def table_kernel(
    core, routes, capacity, spill, tokens, kept, named, limits, features, pick, sem
):
    copies = [
        pltpu.make_async_copy(routes, named, sem.at[0]),
        pltpu.make_async_copy(capacity, limits.at[0:1], sem.at[1]),
        pltpu.make_async_copy(spill, limits.at[1:2], sem.at[2]),
        pltpu.make_async_copy(tokens, features, sem.at[3]),
    ]
    for copy in copies:
        copy.start()
    for copy in copies[:3]:
        copy.wait()
    rank = ranks(named[...], limits[0:1, :], limits[1:2, :])
    experts, count = rank.shape
    slot = lax.broadcasted_iota(jnp.int32, (experts, HALF, count), 1) + core[0] * HALF
    chosen = jnp.where(rank[:, None, :] == slot.astype(jnp.float32), 1.0, 0.0)
    pick[...] = chosen.reshape(experts * HALF, count).astype(jnp.bfloat16)
    copies[3].wait()
    size = experts * HALF
    stores = [
        pltpu.make_async_copy(pick, kept.at[pl.ds(0, size)], sem.at[4]),
        pltpu.make_async_copy(features, kept.at[pl.ds(size, features.shape[0])], sem.at[5]),
    ]
    for copy in stores:
        copy.start()
    for copy in stores:
        copy.wait()


def pick_kernel(kept, tokens_other, rows, pick, features, held, sem):
    size = pick.shape[0]
    depth = tokens_other.shape[0]
    loads = [
        pltpu.make_async_copy(kept.at[pl.ds(0, size)], pick, sem.at[PIECES]),
        pltpu.make_async_copy(
            kept.at[pl.ds(size, depth)], features.at[pl.ds(0, depth)], sem.at[PIECES + 1]
        ),
    ]
    for copy in loads:
        copy.start()
    features[depth:, :] = tokens_other[...]
    for copy in loads:
        copy.wait()
    piece = size // PIECES
    copies = []
    for k in range(PIECES):
        at = pl.ds(k * piece, piece)
        picked = lax.dot_general(
            pick[at, :], features[...], NT, preferred_element_type=jnp.float32
        )
        held[at, :] = picked.astype(jnp.bfloat16)
        copies.append(pltpu.make_async_copy(held.at[at], rows.at[at], sem.at[k]))
        copies[-1].start()
    for copy in copies:
        copy.wait()


def weigh_kernel(routes, weights, capacity, spill, weigh):
    rank = ranks(routes[...], capacity[...], spill[...])
    experts, count = rank.shape
    value = weights[...].astype(jnp.float32)
    share = value / jnp.sum(value, axis=0, keepdims=True)
    number = lax.broadcasted_iota(jnp.int32, (experts, count), 0)
    share_of = jnp.zeros((experts, count), jnp.float32)
    for k in range(value.shape[0]):
        share_of = share_of + jnp.where(routes[k : k + 1, :] == number, share[k : k + 1, :], 0.0)
    slot = lax.broadcasted_iota(jnp.int32, (experts, HALF, count), 1).astype(jnp.float32)
    for half in range(2):
        table = jnp.where(rank[:, None, :] == slot + half * HALF, share_of[:, None, :], 0.0)
        table = table.reshape(experts * HALF, count).T
        upper = table.astype(jnp.bfloat16)
        lower = (table - upper.astype(jnp.float32)).astype(jnp.bfloat16)
        weigh[half, 0:count, :] = upper
        weigh[half, count : 2 * count, :] = lower


def gather_kernel(gate, gate_other, up, up_other, weights, held, came, went):
    loads, stores = [], []
    for n, source in enumerate((gate, gate_other, up, up_other)):
        loads.append(pltpu.make_async_copy(source, held.at[n], came.at[n]))
        loads[-1].start()
    for n, load in enumerate(loads):
        load.wait()
        stores.append(pltpu.make_async_copy(held.at[n], weights.at[n], went.at[n]))
        stores[-1].start()
    for store in stores:
        store.wait()


def project_kernel(parts, chips, rows, weights, *refs):
    outs, (picked, weight, came) = refs[:-3], refs[-3:]
    features = rows.shape[1] // 2
    strips = weights.shape[2] // STRIP
    sources = ((0, 0), (1, 0), (0, 1), (1, 1))
    fetched = []
    for strip in range(strips):
        for n, (low, kind) in enumerate(sources):
            copy = pltpu.make_async_copy(
                weights.at[n, :, pl.ds(strip * STRIP, STRIP)],
                weight.at[strip, pl.ds(low * features, features), pl.ds(kind * STRIP, STRIP)],
                came.at[strip * len(sources) + n],
            )
            copy.start()
            fetched.append(copy)
    depth = picked.shape[0] // len(parts)
    for n, (chip, _) in enumerate(parts):
        start = pl.multiple_of(chips[chip] * depth, depth)
        picked[n * depth : (n + 1) * depth, :] = rows[pl.ds(start, depth), :]
    for strip in range(strips):
        for copy in fetched[strip * len(sources) : (strip + 1) * len(sources)]:
            copy.wait()
        value = jnp.dot(picked[...], weight[strip], preferred_element_type=jnp.float32)
        value = value.astype(jnp.bfloat16)
        at = slice(strip * 2 * STRIP, (strip + 1) * 2 * STRIP)
        out = iter(outs)
        for n, (_, sizes) in enumerate(parts):
            low = n * depth
            for size in sizes:
                next(out)[:, at] = value[low : low + size]
                low += size


def hidden_kernel(*refs):
    terms, hidden = refs[:-1], refs[-1]
    for strip in range(hidden.shape[1] // STRIP):
        at = 2 * STRIP * strip
        gate = jnp.zeros((hidden.shape[0], STRIP), jnp.float32)
        up = gate
        for term in terms:
            gate = gate + term[:, at : at + STRIP].astype(jnp.float32)
            up = up + term[:, at + STRIP : at + 2 * STRIP].astype(jnp.float32)
        value = gate / (1.0 + jnp.exp(-gate)) * up
        hidden[:, STRIP * strip : STRIP * (strip + 1)] = value.astype(jnp.bfloat16)


def down_kernel(places, parts, down, out, held, sem, first):
    depth = held.shape[1]
    features = down.shape[0]
    copies = []
    for part, chips in parts:
        value = lax.dot_general(part, down[...], NT, preferred_element_type=jnp.float32)
        value = value.astype(jnp.bfloat16)
        for n, chip in enumerate(chips):
            low = value[2 * n * depth : (2 * n + 1) * depth]
            high = value[(2 * n + 1) * depth : (2 * n + 2) * depth]
            swapped = places[1, chip] == 1
            slot = chip - first
            held[slot, :, 0:features] = jnp.where(swapped, high, low)
            held[slot, :, features : 2 * features] = jnp.where(swapped, low, high)
            place = pl.multiple_of(places[0, chip] * depth, depth)
            copies.append(
                pltpu.make_async_copy(held.at[slot], out.at[pl.ds(place, depth)], sem.at[slot])
            )
            copies[-1].start()
    for copy in copies:
        copy.wait()


def early_kernel(places, own, near, far, swapped_pair, down, out, held, sem):
    rows = jnp.concatenate([own[...], near[...], far[...]], axis=0)
    parts = ((rows, (0, 1, 2)), (swapped_pair[...], (3, 4)))
    down_kernel(places, parts, down, out, held, sem, 0)


def late_kernel(places, third, fourth, swapped, down, filled, out, held, sem):
    del filled
    depth = fourth.shape[0]
    rows = jnp.concatenate(
        [third[...], swapped[0 : 2 * depth], fourth[...], swapped[2 * depth : 3 * depth]], axis=0
    )
    down_kernel(places, ((rows, (5, 6, 7)),), down, out, held, sem, 5)


def mix_kernel(weigh, values, mixed):
    features, count = mixed.shape
    total = jnp.zeros((features, count), jnp.float32)
    for half in range(2):
        part = jnp.dot(weigh[half], values[...], preferred_element_type=jnp.float32)
        part = (part[:count] + part[count:]).T
        total = total + part[half * features : (half + 1) * features]
    mixed[...] = total.astype(jnp.bfloat16)


def cost(flops, moved):
    return pl.CostEstimate(flops=flops, bytes_accessed=moved, transcendentals=0)


def on_device(
    tokens, routes, weights_int, capacity, spill_size, gate_weight, up_weight, down_weight
):
    experts = capacity.shape[0]
    groups = lax.axis_size("ep")
    planes = lax.axis_size("dp") // 2
    count, features = tokens.shape
    units = gate_weight.shape[2]
    bf16 = jnp.bfloat16
    core = (lax.axis_index("dp") % 2).astype(jnp.int32).reshape(1)
    swap = [(i, i ^ 1) for i in range(2 * planes)]

    own_tokens = tokens.T
    own_routes = routes.T
    own_weights = weights_int.T
    cap_row = capacity.reshape(1, experts)
    spill_row = spill_size.reshape(1, experts)
    gate = gate_weight[0]
    up = up_weight[0]
    down = down_weight[0].T

    tokens_other = lax.ppermute(own_tokens, "dp", swap)
    gate_other = lax.ppermute(gate, "dp", swap)
    up_other = lax.ppermute(up, "dp", swap)

    kept = pl.pallas_call(
        table_kernel,
        out_shape=jax.ShapeDtypeStruct((ROOM, count), bf16),
        in_specs=[SMEM] + [HBM] * 4,
        out_specs=HBM,
        scratch_shapes=[
            pltpu.VMEM(own_routes.shape, jnp.int32),
            pltpu.VMEM((2, experts), jnp.int32),
            pltpu.VMEM((features, count), bf16),
            pltpu.VMEM((experts * HALF, count), bf16),
            pltpu.SemaphoreType.DMA((6,)),
        ],
        compiler_params=pltpu.CompilerParams(vmem_limit_bytes=60 * 1024 * 1024),
        cost_estimate=cost(2 * experts * count * count, 600000),
        name="pick_table",
    )(core, own_routes, cap_row, spill_row, own_tokens)
    send = pl.pallas_call(
        pick_kernel,
        out_shape=jax.ShapeDtypeStruct((experts * HALF, 2 * features), bf16),
        in_specs=[HBM, VMEM],
        out_specs=HBM,
        scratch_shapes=[
            pltpu.VMEM((experts * HALF, count), bf16),
            pltpu.VMEM((2 * features, count), bf16),
            pltpu.VMEM((experts * HALF, 2 * features), bf16),
            pltpu.SemaphoreType.DMA((PIECES + 2,)),
        ],
        compiler_params=pltpu.CompilerParams(vmem_limit_bytes=48 * 1024 * 1024),
        cost_estimate=cost(2 * experts * HALF * count * 2 * features, 2000000),
        name="pick_rows",
    )(kept, tokens_other)
    got = lax.all_to_all(
        send.reshape(groups, HALF, 2 * features), "ep", split_axis=0, concat_axis=0, tiled=True
    ).reshape(groups * HALF, 2 * features)

    depth = groups * HALF
    weights = pl.pallas_call(
        gather_kernel,
        out_shape=jax.ShapeDtypeStruct((HELD,) + gate.shape, bf16),
        in_specs=[HBM] * 4,
        out_specs=HBM,
        scratch_shapes=[
            pltpu.VMEM((4,) + gate.shape, bf16),
            pltpu.SemaphoreType.DMA((4,)),
            pltpu.SemaphoreType.DMA((4,)),
        ],
        compiler_params=LIMIT,
        cost_estimate=cost(0, 7400000),
        name="gather_weights",
    )(gate, gate_other, up, up_other)
    strips = units // STRIP
    part = depth // planes
    half = part // 2
    plane = lax.axis_index("dp") // 2
    chips = jnp.stack([(plane + k) % planes for k in range(planes)]).astype(jnp.int32)

    def project(parts, name):
        shapes = [
            jax.ShapeDtypeStruct((size, 2 * units), bf16) for _, sizes in parts for size in sizes
        ]
        held = len(parts) * part
        return pl.pallas_call(
            functools.partial(project_kernel, parts),
            out_shape=shapes,
            in_specs=[SMEM, VMEM, HBM],
            out_specs=[VMEM] * len(shapes),
            scratch_shapes=[
                pltpu.VMEM((held, 2 * features), bf16),
                pltpu.VMEM((strips, 2 * features, 2 * STRIP), bf16),
                pltpu.SemaphoreType.DMA((4 * strips,)),
            ],
            compiler_params=pltpu.CompilerParams(vmem_limit_bytes=48 * 1024 * 1024),
            cost_estimate=cost(2 * held * 2 * features * 2 * units, 6000000),
            name=name,
        )(chips, got, weights)

    def hop(rows, hops):
        steps = [
            (2 * z + c, 2 * ((z + hops) % planes) + c) for z in range(planes) for c in range(2)
        ]
        return lax.ppermute(rows, "dp", steps)

    def add(*terms):
        return sum(term.astype(jnp.float32) for term in terms).astype(bf16)

    up3, down3, up4, down4 = project(
        ((3, (part,)), (planes - 3, (part,)), (4, (half, half))), "project_in_far"
    )
    here, up1, down1, up2, down2 = project(
        tuple((k % planes, (part,)) for k in (0, 1, -1, 2, -2)), "project_in_near"
    )
    rest = jnp.zeros((half, 2 * units), bf16)
    up2 = add(up2, hop(up3, 1), jnp.concatenate([hop(up4, 2), rest]))
    down2 = add(down2, hop(down3, -1), jnp.concatenate([rest, hop(down4, -2)]))
    terms = (here, hop(up1, 1), hop(down1, -1), hop(up2, 2), hop(down2, -2))
    weigh = pl.pallas_call(
        weigh_kernel,
        out_shape=jax.ShapeDtypeStruct((2, 2 * count, experts * HALF), bf16),
        in_specs=[VMEM] * 4,
        out_specs=VMEM,
        compiler_params=LIMIT,
        cost_estimate=cost(2 * experts * count * count, 4000000),
        name="weigh_table",
    )(own_routes, own_weights, cap_row, spill_row)
    hidden = pl.pallas_call(
        hidden_kernel,
        out_shape=jax.ShapeDtypeStruct((part, units), bf16),
        in_specs=[VMEM] * len(terms),
        out_specs=VMEM,
        compiler_params=LIMIT,
        cost_estimate=cost(8 * part * units, 2200000),
        name="hidden_units",
    )(*terms)

    def flow(rows, hops):
        steps = [
            (2 * z + c, 2 * ((z + (hops, -hops)[c]) % planes) + c)
            for z in range(planes)
            for c in range(2)
        ]
        return lax.ppermute(rows, "dp", steps)

    own = jnp.concatenate([hidden, lax.ppermute(hidden, "dp", swap)], axis=0)
    near, far = flow(own, 1), flow(own, 2)
    third, fourth = flow(far, 1), flow(far[:part], 2)
    swapped_pair = lax.ppermute(jnp.concatenate([near, far], axis=0), "dp", swap)
    swapped_last = lax.ppermute(jnp.concatenate([third, fourth], axis=0), "dp", swap)
    sense = 2 * core[0] - 1
    offsets = [0, sense, 2 * sense, -sense, -2 * sense, 3 * sense, -3 * sense, 4]
    orders = [core[0]] * 3 + [1 - core[0]] * 2 + [core[0], 1 - core[0], core[0]]
    places = jnp.stack(
        [jnp.stack([(plane + chip + planes) % planes for chip in offsets]), jnp.stack(orders)]
    ).astype(jnp.int32)
    back_shape = jax.ShapeDtypeStruct((depth, 2 * features), bf16)

    def scratch(held):
        return [
            pltpu.VMEM((held, part, 2 * features), bf16),
            pltpu.SemaphoreType.DMA((held,)),
        ]

    back = pl.pallas_call(
        early_kernel,
        out_shape=back_shape,
        in_specs=[SMEM] + [VMEM] * 5,
        out_specs=HBM,
        scratch_shapes=scratch(5),
        compiler_params=LIMIT,
        cost_estimate=cost(20 * part * units * features, 4000000),
        name="project_out_early",
    )(places, own, near, far, swapped_pair, down)
    back = pl.pallas_call(
        late_kernel,
        out_shape=back_shape,
        in_specs=[SMEM] + [VMEM] * 4 + [HBM],
        out_specs=HBM,
        scratch_shapes=scratch(3),
        input_output_aliases={5: 0},
        compiler_params=LIMIT,
        cost_estimate=cost(12 * part * units * features, 4000000),
        name="project_out_late",
    )(places, third, fourth, swapped_last, down, back)
    back = back.reshape(groups, HALF, 2 * features)
    values = lax.all_to_all(back, "ep", split_axis=0, concat_axis=0, tiled=True)
    mixed = pl.pallas_call(
        mix_kernel,
        out_shape=jax.ShapeDtypeStruct((features, count), bf16),
        in_specs=[VMEM] * 2,
        out_specs=VMEM,
        compiler_params=LIMIT,
        cost_estimate=cost(8 * count * experts * HALF * 2 * features, 3000000),
        name="mix_rows",
    )(weigh, values.reshape(experts * HALF, 2 * features))
    return mixed.T


def solution(mesh):
    placed = (
        P("ep", "dp"),
        P("ep", None),
        P("ep", None),
        P(),
        P(),
        P("ep", "dp", None),
        P("ep", "dp", None),
        P("ep", None, "dp"),
    )
    return jax.shard_map(
        on_device, mesh=mesh, in_specs=placed, out_specs=P("ep", "dp"), check_vma=False
    )
```

```python
import functools

import jax
import jax.numpy as jnp
from jax import lax
from jax.experimental import pallas as pl
from jax.experimental.pallas import tpu as pltpu
from jax.sharding import PartitionSpec as P

HALF = 24
HELD = 20
ORDER = (3, 4, 2, 1, 0)
FAR, NEAR = ORDER[:2], ORDER[2:]
PIECES = 4
STRIP = 256

VMEM = pl.BlockSpec(memory_space=pltpu.VMEM)
SMEM = pl.BlockSpec(memory_space=pltpu.SMEM)
NT = (((1,), (1,)), ((), ()))
HBM = pl.BlockSpec(memory_space=pltpu.HBM)
LIMIT = pltpu.CompilerParams(vmem_limit_bytes=40 * 1024 * 1024)
LARGE = pltpu.CompilerParams(vmem_limit_bytes=60 * 1024 * 1024)


def column(row, experts):
    first = lax.broadcasted_iota(jnp.int32, (experts, experts), 0)
    second = lax.broadcasted_iota(jnp.int32, (experts, experts), 1)
    spread = jnp.where(first == second, jnp.broadcast_to(row, (experts, experts)), 0.0)
    return jnp.sum(spread, axis=1, keepdims=True)


def ranks(routes, capacity, spill):
    experts = capacity.shape[1]
    top, tokens = routes.shape
    number = lax.broadcasted_iota(jnp.int32, (experts, tokens), 0)
    named = jnp.zeros((experts, tokens), jnp.float32)
    for k in range(top):
        named = named + jnp.where(routes[k : k + 1, :] == number, 1.0, 0.0)
    earlier = lax.broadcasted_iota(jnp.int32, (tokens, tokens), 0) < lax.broadcasted_iota(
        jnp.int32, (tokens, tokens), 1
    )
    before = jnp.dot(
        named.astype(jnp.bfloat16),
        jnp.where(earlier, 1.0, 0.0).astype(jnp.bfloat16),
        preferred_element_type=jnp.float32,
    )
    limit = column((capacity + spill).astype(jnp.float32), experts)
    return jnp.where((named > 0.0) & (before < limit), before, -1.0)


def pick_kernel(routes, capacity, spill, tokens, rows, named, limits, features, held, sem):
    copies = [
        pltpu.make_async_copy(routes, named, sem.at[0]),
        pltpu.make_async_copy(capacity, limits.at[0:1], sem.at[1]),
        pltpu.make_async_copy(spill, limits.at[1:2], sem.at[2]),
        pltpu.make_async_copy(tokens, features, sem.at[3]),
    ]
    for copy in copies:
        copy.start()
    for copy in copies[:3]:
        copy.wait()
    rank = ranks(named[...], limits[0:1, :], limits[1:2, :])
    experts, count = rank.shape
    slot = lax.broadcasted_iota(jnp.int32, (experts, HALF, count), 1).astype(jnp.float32)
    copies[3].wait()
    width = features.shape[0]
    piece = experts * HALF // PIECES
    picks = []
    for half in range(2):
        chosen = jnp.where(rank[:, None, :] == slot + half * HALF, 1.0, 0.0)
        picks.append(chosen.reshape(experts * HALF, count).astype(jnp.bfloat16))
    stores = []
    for k in range(PIECES):
        at = pl.ds(k * piece, piece)
        for half in range(2):
            picked = lax.dot_general(
                picks[half][k * piece : (k + 1) * piece],
                features[...],
                NT,
                preferred_element_type=jnp.float32,
            )
            held[at, half * width : (half + 1) * width] = picked.astype(jnp.bfloat16)
        stores.append(pltpu.make_async_copy(held.at[at], rows.at[at], sem.at[4 + k]))
        stores[-1].start()
    for copy in stores:
        copy.wait()


def weigh_kernel(routes, weights, capacity, spill, weigh):
    rank = ranks(routes[...], capacity[...], spill[...])
    experts, count = rank.shape
    value = weights[...].astype(jnp.float32)
    share = value / jnp.sum(value, axis=0, keepdims=True)
    number = lax.broadcasted_iota(jnp.int32, (experts, count), 0)
    share_of = jnp.zeros((experts, count), jnp.float32)
    for k in range(value.shape[0]):
        share_of = share_of + jnp.where(routes[k : k + 1, :] == number, share[k : k + 1, :], 0.0)
    slot = lax.broadcasted_iota(jnp.int32, (experts, HALF, count), 1).astype(jnp.float32)
    for half in range(2):
        table = jnp.where(rank[:, None, :] == slot + half * HALF, share_of[:, None, :], 0.0)
        table = table.reshape(experts * HALF, count).T
        upper = table.astype(jnp.bfloat16)
        lower = (table - upper.astype(jnp.float32)).astype(jnp.bfloat16)
        weigh[half, 0:count, :] = upper
        weigh[half, count : 2 * count, :] = lower


def gather_kernel(gate, gate_other, up, up_other, weights, held, came, went):
    loads, stores = [], []
    for n, source in enumerate((gate, gate_other, up, up_other)):
        loads.append(pltpu.make_async_copy(source, held.at[n], came.at[n]))
        loads[-1].start()
    for n, load in enumerate(loads):
        load.wait()
        stores.append(pltpu.make_async_copy(held.at[n], weights.at[n], went.at[n]))
        stores[-1].start()
    for store in stores:
        store.wait()


def held_rows(chip, part):
    return part // 2 if chip in (0, 4) else part


def order_kernel(rows, after, same):
    del rows, after, same


def project_kernel(places, rows, taken, weights, *refs, chips, part):
    outs, (picked, weight, came) = refs[:-3], refs[-3:]
    features = rows.shape[1] // 2
    strips = weights.shape[2] // STRIP
    sources = ((0, 0), (1, 0), (0, 1), (1, 1))
    fetched = []
    for strip in range(strips):
        for n, (low, kind) in enumerate(sources):
            copy = pltpu.make_async_copy(
                weights.at[n, :, pl.ds(strip * STRIP, STRIP)],
                weight.at[strip, pl.ds(low * features, features), pl.ds(kind * STRIP, STRIP)],
                came.at[strip * len(sources) + n],
            )
            copy.start()
            fetched.append(copy)
    low = 0
    for chip in chips:
        size = held_rows(chip, part)
        start = pl.multiple_of(places[chip], part // 2)
        own = rows[pl.ds(start, size), :]
        other = taken[pl.ds(start, size), :]
        for half in range(2):
            at = slice(low, low + size)
            lanes = slice(half * features, (half + 1) * features)
            picked[at, 0:features] = own[:, lanes]
            picked[at, features : 2 * features] = other[:, lanes]
            low += size
    for strip in range(strips):
        for copy in fetched[strip * len(sources) : (strip + 1) * len(sources)]:
            copy.wait()
        value = jnp.dot(picked[...], weight[strip], preferred_element_type=jnp.float32)
        value = value.astype(jnp.bfloat16)
        low = 0
        for chip, out in zip(chips, outs):
            size = 2 * held_rows(chip, part)
            out[:, strip * 2 * STRIP : (strip + 1) * 2 * STRIP] = value[low : low + size]
            low += size


def add_kernel(core, first, second, half, total):
    size = half.shape[0] // 2
    low = core[0] == 0
    for n in range(2):
        for blocks in range(2):
            at = slice((2 * n + blocks) * size, (2 * n + blocks + 1) * size)
            value = first[at, :].astype(jnp.float32) + second[at, :].astype(jnp.float32)
            more = half[n * size : (n + 1) * size, :].astype(jnp.float32)
            mine = low if blocks == 0 else jnp.logical_not(low)
            total[at, :] = jnp.where(mine, value + more, value).astype(jnp.bfloat16)


def hidden_kernel(*refs):
    terms, hidden = refs[:-1], refs[-1]
    for strip in range(hidden.shape[1] // STRIP):
        at = 2 * STRIP * strip
        gate = jnp.zeros((hidden.shape[0], STRIP), jnp.float32)
        up = gate
        for term in terms:
            gate = gate + term[:, at : at + STRIP].astype(jnp.float32)
            up = up + term[:, at + STRIP : at + 2 * STRIP].astype(jnp.float32)
        value = gate / (1.0 + jnp.exp(-gate)) * up
        hidden[:, STRIP * strip : STRIP * (strip + 1)] = value.astype(jnp.bfloat16)


def down_kernel(places, parts, down, out, held, sem, first):
    depth = held.shape[1]
    features = down.shape[0]
    copies = []
    for part, chips in parts:
        value = lax.dot_general(part, down[...], NT, preferred_element_type=jnp.float32)
        value = value.astype(jnp.bfloat16)
        for n, chip in enumerate(chips):
            low = value[2 * n * depth : (2 * n + 1) * depth]
            high = value[(2 * n + 1) * depth : (2 * n + 2) * depth]
            swapped = places[1, chip] == 1
            slot = chip - first
            held[slot, :, 0:features] = jnp.where(swapped, high, low)
            held[slot, :, features : 2 * features] = jnp.where(swapped, low, high)
            place = pl.multiple_of(places[0, chip] * depth, depth)
            copies.append(
                pltpu.make_async_copy(held.at[slot], out.at[pl.ds(place, depth)], sem.at[slot])
            )
            copies[-1].start()
    for copy in copies:
        copy.wait()


def early_kernel(places, own, near, far, swapped_pair, down, out, held, sem):
    rows = jnp.concatenate([own[...], near[...], far[...]], axis=0)
    parts = ((rows, (0, 1, 2)), (swapped_pair[...], (3, 4)))
    down_kernel(places, parts, down, out, held, sem, 0)


def late_kernel(places, third, fourth, swapped, down, filled, out, held, sem):
    del filled
    depth = fourth.shape[0]
    rows = jnp.concatenate(
        [third[...], swapped[0 : 2 * depth], fourth[...], swapped[2 * depth : 3 * depth]], axis=0
    )
    down_kernel(places, ((rows, (5, 6, 7)),), down, out, held, sem, 5)


def mix_kernel(weigh, values, mixed):
    features, count = mixed.shape
    total = jnp.zeros((features, count), jnp.float32)
    for half in range(2):
        part = jnp.dot(weigh[half], values[...], preferred_element_type=jnp.float32)
        part = (part[:count] + part[count:]).T
        total = total + part[half * features : (half + 1) * features]
    mixed[...] = total.astype(jnp.bfloat16)


def cost(flops, moved):
    return pl.CostEstimate(flops=flops, bytes_accessed=moved, transcendentals=0)


def on_device(
    tokens, routes, weights_int, capacity, spill_size, gate_weight, up_weight, down_weight
):
    experts = capacity.shape[0]
    groups = lax.axis_size("ep")
    planes = lax.axis_size("dp") // 2
    count, features = tokens.shape
    units = gate_weight.shape[2]
    bf16 = jnp.bfloat16
    core = (lax.axis_index("dp") % 2).astype(jnp.int32).reshape(1)
    swap = [(i, i ^ 1) for i in range(2 * planes)]

    own_tokens = tokens.T
    own_routes = routes.T
    own_weights = weights_int.T
    cap_row = capacity.reshape(1, experts)
    spill_row = spill_size.reshape(1, experts)
    gate = gate_weight[0]
    up = up_weight[0]
    down = down_weight[0].T

    gate_other = lax.ppermute(gate, "dp", swap)
    up_other = lax.ppermute(up, "dp", swap)

    send = pl.pallas_call(
        pick_kernel,
        out_shape=jax.ShapeDtypeStruct((experts * HALF, 2 * features), bf16),
        in_specs=[HBM] * 4,
        out_specs=HBM,
        scratch_shapes=[
            pltpu.VMEM(own_routes.shape, jnp.int32),
            pltpu.VMEM((2, experts), jnp.int32),
            pltpu.VMEM((features, count), bf16),
            pltpu.VMEM((experts * HALF, 2 * features), bf16),
            pltpu.SemaphoreType.DMA((4 + PIECES,)),
        ],
        compiler_params=pltpu.CompilerParams(vmem_limit_bytes=60 * 1024 * 1024),
        cost_estimate=cost(2 * experts * HALF * count * 2 * features, 2000000),
        name="pick_rows",
    )(own_routes, cap_row, spill_row, own_tokens)
    got = lax.all_to_all(
        send.reshape(groups, HALF, 2 * features), "ep", split_axis=0, concat_axis=0, tiled=True
    ).reshape(groups * HALF, 2 * features)

    depth = groups * HALF
    weights = pl.pallas_call(
        gather_kernel,
        out_shape=jax.ShapeDtypeStruct((HELD,) + gate.shape, bf16),
        in_specs=[HBM] * 4,
        out_specs=HBM,
        scratch_shapes=[
            pltpu.VMEM((4,) + gate.shape, bf16),
            pltpu.SemaphoreType.DMA((4,)),
            pltpu.SemaphoreType.DMA((4,)),
        ],
        compiler_params=LIMIT,
        cost_estimate=cost(0, 7400000),
        name="gather_weights",
    )(gate, gate_other, up, up_other)
    strips = units // STRIP
    part = depth // planes
    plane = lax.axis_index("dp") // 2
    sense = 1 - 2 * core[0]

    places = jnp.stack(
        [
            (plane + sense * k + planes) % planes * part + (core[0] * part // 2 if k in (0, 4) else 0)
            for k in range(5)
        ]
    ).astype(jnp.int32)
    anywhere = pl.BlockSpec(memory_space=pl.ANY)
    got = pl.pallas_call(
        order_kernel,
        out_shape=jax.ShapeDtypeStruct(got.shape, bf16),
        in_specs=[anywhere] * 2,
        out_specs=anywhere,
        input_output_aliases={0: 0},
        compiler_params=LIMIT,
        cost_estimate=cost(0, 1000),
        name="after_weights",
    )(got, weights)
    taken = lax.ppermute(got, "dp", swap)

    def project(chips, name):
        sizes = [2 * held_rows(chip, part) for chip in chips]
        return pl.pallas_call(
            functools.partial(project_kernel, chips=chips, part=part),
            out_shape=[jax.ShapeDtypeStruct((size, 2 * units), bf16) for size in sizes],
            in_specs=[SMEM, VMEM, VMEM, HBM],
            out_specs=[VMEM] * len(sizes),
            scratch_shapes=[
                pltpu.VMEM((sum(sizes), 2 * features), bf16),
                pltpu.VMEM((strips, 2 * features, 2 * STRIP), bf16),
                pltpu.SemaphoreType.DMA((4 * strips,)),
            ],
            compiler_params=pltpu.CompilerParams(vmem_limit_bytes=48 * 1024 * 1024),
            cost_estimate=cost(2 * sum(sizes) * 2 * features * 2 * units, 6000000),
            name=name,
        )(places, got, taken, weights)

    def flow(rows, hops):
        steps = [
            (2 * z + c, 2 * ((z + (hops, -hops)[c]) % planes) + c)
            for z in range(planes)
            for c in range(2)
        ]
        return lax.ppermute(rows, "dp", steps)

    def add(first, second, half, name):
        return pl.pallas_call(
            add_kernel,
            out_shape=jax.ShapeDtypeStruct((2 * part, 2 * units), bf16),
            in_specs=[SMEM] + [VMEM] * 3,
            out_specs=VMEM,
            compiler_params=LIMIT,
            cost_estimate=cost(6 * part * units, 3000000),
            name=name,
        )(core, first, second, half)

    third, fourth = project(FAR, "project_in_far")
    second, first, here = project(NEAR, "project_in_near")
    second = add(second, flow(third, 1), flow(fourth, 2), "add_passing")
    reached = add(flow(first, 1), flow(second, 2), here, "add_reached")
    terms = (reached, lax.ppermute(reached, "dp", swap))
    weigh = pl.pallas_call(
        weigh_kernel,
        out_shape=jax.ShapeDtypeStruct((2, 2 * count, experts * HALF), bf16),
        in_specs=[VMEM] * 4,
        out_specs=VMEM,
        compiler_params=LIMIT,
        cost_estimate=cost(2 * experts * count * count, 4000000),
        name="weigh_table",
    )(own_routes, own_weights, cap_row, spill_row)
    hidden = pl.pallas_call(
        hidden_kernel,
        out_shape=jax.ShapeDtypeStruct((2 * part, units), bf16),
        in_specs=[VMEM] * len(terms),
        out_specs=VMEM,
        compiler_params=LIMIT,
        cost_estimate=cost(8 * part * units, 2000000),
        name="hidden_units",
    )(*terms)

    near, far = flow(hidden, 1), flow(hidden, 2)
    far_half = jnp.where(core[0] == 0, far[:part], far[part:])
    third, fourth = flow(far, 1), flow(far_half, 2)
    swapped_pair = lax.ppermute(jnp.concatenate([near, far], axis=0), "dp", swap)
    swapped_last = lax.ppermute(jnp.concatenate([third, fourth], axis=0), "dp", swap)
    offsets = [0, -sense, -2 * sense, sense, 2 * sense, -3 * sense, 3 * sense, 4]
    orders = [core[0] * 0] * 7 + [core[0]]
    places = jnp.stack(
        [jnp.stack([(plane + chip + planes) % planes for chip in offsets]), jnp.stack(orders)]
    ).astype(jnp.int32)
    back_shape = jax.ShapeDtypeStruct((depth, 2 * features), bf16)

    def scratch(held):
        return [
            pltpu.VMEM((held, part, 2 * features), bf16),
            pltpu.SemaphoreType.DMA((held,)),
        ]

    back = pl.pallas_call(
        early_kernel,
        out_shape=back_shape,
        in_specs=[SMEM] + [VMEM] * 5,
        out_specs=HBM,
        scratch_shapes=scratch(5),
        compiler_params=LIMIT,
        cost_estimate=cost(20 * part * units * features, 4000000),
        name="project_out_early",
    )(places, hidden, near, far, swapped_pair, down)
    back = pl.pallas_call(
        late_kernel,
        out_shape=back_shape,
        in_specs=[SMEM] + [VMEM] * 4 + [HBM],
        out_specs=HBM,
        scratch_shapes=scratch(3),
        input_output_aliases={5: 0},
        compiler_params=LIMIT,
        cost_estimate=cost(12 * part * units * features, 4000000),
        name="project_out_late",
    )(places, third, fourth, swapped_last, down, back)
    back = back.reshape(groups, HALF, 2 * features)
    values = lax.all_to_all(back, "ep", split_axis=0, concat_axis=0, tiled=True)
    mixed = pl.pallas_call(
        mix_kernel,
        out_shape=jax.ShapeDtypeStruct((features, count), bf16),
        in_specs=[VMEM] * 2,
        out_specs=VMEM,
        compiler_params=LIMIT,
        cost_estimate=cost(8 * count * experts * HALF * 2 * features, 3000000),
        name="mix_rows",
    )(weigh, values.reshape(experts * HALF, 2 * features))
    return mixed.T


def solution(mesh):
    placed = (
        P("ep", "dp"),
        P("ep", None),
        P("ep", None),
        P(),
        P(),
        P("ep", "dp", None),
        P("ep", "dp", None),
        P("ep", None, "dp"),
    )
    return jax.shard_map(
        on_device, mesh=mesh, in_specs=placed, out_specs=P("ep", "dp"), check_vma=False
    )
```

```python
import functools

import jax
import jax.numpy as jnp
from jax import lax
from jax.experimental import pallas as pl
from jax.experimental.pallas import tpu as pltpu
from jax.sharding import PartitionSpec as P

HALF = 24
HELD = 20
PIECES = 4
STRIP = 256

VMEM = pl.BlockSpec(memory_space=pltpu.VMEM)
SMEM = pl.BlockSpec(memory_space=pltpu.SMEM)
NT = (((1,), (1,)), ((), ()))
HBM = pl.BlockSpec(memory_space=pltpu.HBM)
LIMIT = pltpu.CompilerParams(vmem_limit_bytes=40 * 1024 * 1024)
LARGE = pltpu.CompilerParams(vmem_limit_bytes=60 * 1024 * 1024)


def column(row, experts):
    first = lax.broadcasted_iota(jnp.int32, (experts, experts), 0)
    second = lax.broadcasted_iota(jnp.int32, (experts, experts), 1)
    spread = jnp.where(first == second, jnp.broadcast_to(row, (experts, experts)), 0.0)
    return jnp.sum(spread, axis=1, keepdims=True)


def ranks(routes, capacity, spill):
    experts = capacity.shape[1]
    top, tokens = routes.shape
    number = lax.broadcasted_iota(jnp.int32, (experts, tokens), 0)
    named = jnp.zeros((experts, tokens), jnp.float32)
    for k in range(top):
        named = named + jnp.where(routes[k : k + 1, :] == number, 1.0, 0.0)
    earlier = lax.broadcasted_iota(jnp.int32, (tokens, tokens), 0) < lax.broadcasted_iota(
        jnp.int32, (tokens, tokens), 1
    )
    before = jnp.dot(
        named.astype(jnp.bfloat16),
        jnp.where(earlier, 1.0, 0.0).astype(jnp.bfloat16),
        preferred_element_type=jnp.float32,
    )
    limit = column((capacity + spill).astype(jnp.float32), experts)
    return jnp.where((named > 0.0) & (before < limit), before, -1.0)


def pick_kernel(routes, capacity, spill, tokens, rows, named, limits, features, held, sem):
    copies = [
        pltpu.make_async_copy(routes, named, sem.at[0]),
        pltpu.make_async_copy(capacity, limits.at[0:1], sem.at[1]),
        pltpu.make_async_copy(spill, limits.at[1:2], sem.at[2]),
        pltpu.make_async_copy(tokens, features, sem.at[3]),
    ]
    for copy in copies:
        copy.start()
    for copy in copies[:3]:
        copy.wait()
    rank = ranks(named[...], limits[0:1, :], limits[1:2, :])
    experts, count = rank.shape
    slot = lax.broadcasted_iota(jnp.int32, (experts, HALF, count), 1).astype(jnp.float32)
    copies[3].wait()
    width = features.shape[0]
    piece = experts * HALF // PIECES
    picks = []
    for half in range(2):
        chosen = jnp.where(rank[:, None, :] == slot + half * HALF, 1.0, 0.0)
        picks.append(chosen.reshape(experts * HALF, count).astype(jnp.bfloat16))
    stores = []
    for k in range(PIECES):
        at = pl.ds(k * piece, piece)
        for half in range(2):
            picked = lax.dot_general(
                picks[half][k * piece : (k + 1) * piece],
                features[...],
                NT,
                preferred_element_type=jnp.float32,
            )
            held[at, half * width : (half + 1) * width] = picked.astype(jnp.bfloat16)
        stores.append(pltpu.make_async_copy(held.at[at], rows.at[at], sem.at[4 + k]))
        stores[-1].start()
    for copy in stores:
        copy.wait()


def weigh_kernel(routes, weights, capacity, spill, weigh):
    rank = ranks(routes[...], capacity[...], spill[...])
    experts, count = rank.shape
    value = weights[...].astype(jnp.float32)
    share = value / jnp.sum(value, axis=0, keepdims=True)
    number = lax.broadcasted_iota(jnp.int32, (experts, count), 0)
    share_of = jnp.zeros((experts, count), jnp.float32)
    for k in range(value.shape[0]):
        share_of = share_of + jnp.where(routes[k : k + 1, :] == number, share[k : k + 1, :], 0.0)
    slot = lax.broadcasted_iota(jnp.int32, (experts, HALF, count), 1).astype(jnp.float32)
    for half in range(2):
        table = jnp.where(rank[:, None, :] == slot + half * HALF, share_of[:, None, :], 0.0)
        table = table.reshape(experts * HALF, count).T
        upper = table.astype(jnp.bfloat16)
        lower = (table - upper.astype(jnp.float32)).astype(jnp.bfloat16)
        weigh[half, 0:count, :] = upper
        weigh[half, count : 2 * count, :] = lower


def gather_kernel(gate, gate_other, up, up_other, weights, held, came, went):
    loads, stores = [], []
    for n, source in enumerate((gate, gate_other, up, up_other)):
        loads.append(pltpu.make_async_copy(source, held.at[n], came.at[n]))
        loads[-1].start()
    for n, load in enumerate(loads):
        load.wait()
        stores.append(pltpu.make_async_copy(held.at[n], weights.at[n], went.at[n]))
        stores[-1].start()
    for store in stores:
        store.wait()


def held_rows(chip, part):
    return part // 2 if chip in (0, 4) else part


def order_kernel(rows, after, same):
    del rows, after, same


def load_kernel(weights, weight, came):
    features = weights.shape[1]
    copies = []
    for strip in range(weight.shape[0]):
        for n, (low, kind) in enumerate(((0, 0), (1, 0), (0, 1), (1, 1))):
            copies.append(
                pltpu.make_async_copy(
                    weights.at[n, :, pl.ds(strip * STRIP, STRIP)],
                    weight.at[strip, pl.ds(low * features, features), pl.ds(kind * STRIP, STRIP)],
                    came.at[4 * strip + n],
                )
            )
    for copy in copies:
        copy.start()
    for copy in copies:
        copy.wait()


def project_kernel(places, rows, taken, weight, *refs, chips, part):
    outs, picked = refs[:-1], refs[-1]
    features = rows.shape[1] // 2
    low = 0
    for chip in chips:
        size = held_rows(chip, part)
        start = pl.multiple_of(places[chip], part // 2)
        own = rows[pl.ds(start, size), :]
        other = taken[pl.ds(start, size), :]
        for half in range(2):
            at = slice(low, low + size)
            lanes = slice(half * features, (half + 1) * features)
            picked[at, 0:features] = own[:, lanes]
            picked[at, features : 2 * features] = other[:, lanes]
            low += size
    for strip in range(weight.shape[0]):
        value = jnp.dot(picked[...], weight[strip], preferred_element_type=jnp.float32)
        value = value.astype(jnp.bfloat16)
        low = 0
        for chip, out in zip(chips, outs):
            size = 2 * held_rows(chip, part)
            out[:, strip * 2 * STRIP : (strip + 1) * 2 * STRIP] = value[low : low + size]
            low += size


def add_kernel(core, first, second, half, total):
    size = half.shape[0] // 2
    low = core[0] == 0
    for n in range(2):
        for blocks in range(2):
            at = slice((2 * n + blocks) * size, (2 * n + blocks + 1) * size)
            value = first[at, :].astype(jnp.float32) + second[at, :].astype(jnp.float32)
            more = half[n * size : (n + 1) * size, :].astype(jnp.float32)
            mine = low if blocks == 0 else jnp.logical_not(low)
            total[at, :] = jnp.where(mine, value + more, value).astype(jnp.bfloat16)


def hidden_kernel(*refs):
    terms, hidden = refs[:-1], refs[-1]
    for strip in range(hidden.shape[1] // STRIP):
        at = 2 * STRIP * strip
        gate = jnp.zeros((hidden.shape[0], STRIP), jnp.float32)
        up = gate
        for term in terms:
            gate = gate + term[:, at : at + STRIP].astype(jnp.float32)
            up = up + term[:, at + STRIP : at + 2 * STRIP].astype(jnp.float32)
        value = gate / (1.0 + jnp.exp(-gate)) * up
        hidden[:, STRIP * strip : STRIP * (strip + 1)] = value.astype(jnp.bfloat16)


def down_kernel(places, parts, down, out, held, sem, first):
    depth = held.shape[1]
    features = down.shape[0]
    copies = []
    for part, chips in parts:
        value = lax.dot_general(part, down[...], NT, preferred_element_type=jnp.float32)
        value = value.astype(jnp.bfloat16)
        for n, chip in enumerate(chips):
            low = value[2 * n * depth : (2 * n + 1) * depth]
            high = value[(2 * n + 1) * depth : (2 * n + 2) * depth]
            swapped = places[1, chip] == 1
            slot = chip - first
            held[slot, :, 0:features] = jnp.where(swapped, high, low)
            held[slot, :, features : 2 * features] = jnp.where(swapped, low, high)
            place = pl.multiple_of(places[0, chip] * depth, depth)
            copies.append(
                pltpu.make_async_copy(held.at[slot], out.at[pl.ds(place, depth)], sem.at[slot])
            )
            copies[-1].start()
    for copy in copies:
        copy.wait()


def early_kernel(places, own, near, far, swapped_pair, third, down, out, held, sem):
    rows = [term[...] for term in (own, near, far, swapped_pair, third)]
    rows = jnp.concatenate(rows, axis=0)
    down_kernel(places, ((rows, (0, 1, 2, 3, 4, 5)),), down, out, held, sem, 0)


def late_kernel(places, fourth, swapped, down, filled, out, held, sem):
    del filled
    depth = fourth.shape[0]
    rows = jnp.concatenate(
        [swapped[0 : 2 * depth], fourth[...], swapped[2 * depth : 3 * depth]], axis=0
    )
    down_kernel(places, ((rows, (6, 7)),), down, out, held, sem, 6)


def mix_kernel(weigh, values, mixed):
    features, count = mixed.shape
    total = jnp.zeros((features, count), jnp.float32)
    for half in range(2):
        part = jnp.dot(weigh[half], values[...], preferred_element_type=jnp.float32)
        part = (part[:count] + part[count:]).T
        total = total + part[half * features : (half + 1) * features]
    mixed[...] = total.astype(jnp.bfloat16)


def cost(flops, moved):
    return pl.CostEstimate(flops=flops, bytes_accessed=moved, transcendentals=0)


def on_device(
    tokens, routes, weights_int, capacity, spill_size, gate_weight, up_weight, down_weight
):
    experts = capacity.shape[0]
    groups = lax.axis_size("ep")
    planes = lax.axis_size("dp") // 2
    count, features = tokens.shape
    units = gate_weight.shape[2]
    bf16 = jnp.bfloat16
    core = (lax.axis_index("dp") % 2).astype(jnp.int32).reshape(1)
    swap = [(i, i ^ 1) for i in range(2 * planes)]

    own_tokens = tokens.T
    own_routes = routes.T
    own_weights = weights_int.T
    cap_row = capacity.reshape(1, experts)
    spill_row = spill_size.reshape(1, experts)
    gate = gate_weight[0]
    up = up_weight[0]
    down = down_weight[0].T

    gate_other = lax.ppermute(gate, "dp", swap)
    up_other = lax.ppermute(up, "dp", swap)

    send = pl.pallas_call(
        pick_kernel,
        out_shape=jax.ShapeDtypeStruct((experts * HALF, 2 * features), bf16),
        in_specs=[HBM] * 4,
        out_specs=HBM,
        scratch_shapes=[
            pltpu.VMEM(own_routes.shape, jnp.int32),
            pltpu.VMEM((2, experts), jnp.int32),
            pltpu.VMEM((features, count), bf16),
            pltpu.VMEM((experts * HALF, 2 * features), bf16),
            pltpu.SemaphoreType.DMA((4 + PIECES,)),
        ],
        compiler_params=pltpu.CompilerParams(vmem_limit_bytes=60 * 1024 * 1024),
        cost_estimate=cost(2 * experts * HALF * count * 2 * features, 2000000),
        name="pick_rows",
    )(own_routes, cap_row, spill_row, own_tokens)
    got = lax.all_to_all(
        send.reshape(groups, HALF, 2 * features), "ep", split_axis=0, concat_axis=0, tiled=True
    ).reshape(groups * HALF, 2 * features)

    depth = groups * HALF
    weights = pl.pallas_call(
        gather_kernel,
        out_shape=jax.ShapeDtypeStruct((HELD,) + gate.shape, bf16),
        in_specs=[HBM] * 4,
        out_specs=HBM,
        scratch_shapes=[
            pltpu.VMEM((4,) + gate.shape, bf16),
            pltpu.SemaphoreType.DMA((4,)),
            pltpu.SemaphoreType.DMA((4,)),
        ],
        compiler_params=LIMIT,
        cost_estimate=cost(0, 7400000),
        name="gather_weights",
    )(gate, gate_other, up, up_other)
    strips = units // STRIP
    part = depth // planes
    plane = lax.axis_index("dp") // 2
    sense = 1 - 2 * core[0]

    places = jnp.stack(
        [
            (plane + sense * k + planes) % planes * part + (core[0] * part // 2 if k in (0, 4) else 0)
            for k in range(5)
        ]
    ).astype(jnp.int32)
    anywhere = pl.BlockSpec(memory_space=pl.ANY)
    got = pl.pallas_call(
        order_kernel,
        out_shape=jax.ShapeDtypeStruct(got.shape, bf16),
        in_specs=[anywhere] * 2,
        out_specs=anywhere,
        input_output_aliases={0: 0},
        compiler_params=LIMIT,
        cost_estimate=cost(0, 1000),
        name="after_weights",
    )(got, weights)
    taken = lax.ppermute(got, "dp", swap)
    weight = pl.pallas_call(
        load_kernel,
        out_shape=jax.ShapeDtypeStruct((strips, 2 * features, 2 * STRIP), bf16),
        in_specs=[HBM],
        out_specs=VMEM,
        scratch_shapes=[pltpu.SemaphoreType.DMA((4 * strips,))],
        compiler_params=pltpu.CompilerParams(vmem_limit_bytes=48 * 1024 * 1024),
        cost_estimate=cost(0, 7400000),
        name="load_weights",
    )(weights)

    def project(chips, name):
        sizes = [2 * held_rows(chip, part) for chip in chips]
        return pl.pallas_call(
            functools.partial(project_kernel, chips=chips, part=part),
            out_shape=[jax.ShapeDtypeStruct((size, 2 * units), bf16) for size in sizes],
            in_specs=[SMEM] + [VMEM] * 3,
            out_specs=[VMEM] * len(sizes),
            scratch_shapes=[pltpu.VMEM((sum(sizes), 2 * features), bf16)],
            compiler_params=LIMIT,
            cost_estimate=cost(2 * sum(sizes) * 2 * features * 2 * units, 6000000),
            name=name,
        )(places, got, taken, weight)

    def flow(rows, hops):
        steps = [
            (2 * z + c, 2 * ((z + (hops, -hops)[c]) % planes) + c)
            for z in range(planes)
            for c in range(2)
        ]
        return lax.ppermute(rows, "dp", steps)

    def add(first, second, half, name):
        return pl.pallas_call(
            add_kernel,
            out_shape=jax.ShapeDtypeStruct((2 * part, 2 * units), bf16),
            in_specs=[SMEM] + [VMEM] * 3,
            out_specs=VMEM,
            compiler_params=LIMIT,
            cost_estimate=cost(6 * part * units, 3000000),
            name=name,
        )(core, first, second, half)

    (fourth,) = project((4,), "project_in_opposite")
    (third,) = project((3,), "project_in_third")
    second, first, here = project((2, 1, 0), "project_in_near")
    second = add(second, flow(third, 1), flow(fourth, 2), "add_passing")
    reached = add(flow(first, 1), flow(second, 2), here, "add_reached")
    terms = (reached, lax.ppermute(reached, "dp", swap))
    weigh = pl.pallas_call(
        weigh_kernel,
        out_shape=jax.ShapeDtypeStruct((2, 2 * count, experts * HALF), bf16),
        in_specs=[VMEM] * 4,
        out_specs=VMEM,
        compiler_params=LIMIT,
        cost_estimate=cost(2 * experts * count * count, 4000000),
        name="weigh_table",
    )(own_routes, own_weights, cap_row, spill_row)
    hidden = pl.pallas_call(
        hidden_kernel,
        out_shape=jax.ShapeDtypeStruct((2 * part, units), bf16),
        in_specs=[VMEM] * len(terms),
        out_specs=VMEM,
        compiler_params=LIMIT,
        cost_estimate=cost(8 * part * units, 2000000),
        name="hidden_units",
    )(*terms)

    near, far = flow(hidden, 1), flow(hidden, 2)
    far_half = jnp.where(core[0] == 0, far[:part], far[part:])
    third, fourth = flow(far, 1), flow(far_half, 2)
    swapped_pair = lax.ppermute(jnp.concatenate([near, far], axis=0), "dp", swap)
    swapped_last = lax.ppermute(jnp.concatenate([third, fourth], axis=0), "dp", swap)
    offsets = [0, -sense, -2 * sense, sense, 2 * sense, -3 * sense, 3 * sense, 4]
    orders = [core[0] * 0] * 7 + [core[0]]
    places = jnp.stack(
        [jnp.stack([(plane + chip + planes) % planes for chip in offsets]), jnp.stack(orders)]
    ).astype(jnp.int32)
    back_shape = jax.ShapeDtypeStruct((depth, 2 * features), bf16)

    def scratch(held):
        return [
            pltpu.VMEM((held, part, 2 * features), bf16),
            pltpu.SemaphoreType.DMA((held,)),
        ]

    def project_back(kernel, held, rows, filled, name):
        return pl.pallas_call(
            kernel,
            out_shape=back_shape,
            in_specs=[SMEM] + [VMEM] * (len(rows) + 1) + [HBM] * len(filled),
            out_specs=HBM,
            scratch_shapes=scratch(held),
            input_output_aliases={len(rows) + 2: 0} if filled else {},
            compiler_params=LIMIT,
            cost_estimate=cost(4 * held * part * units * features, 3000000),
            name=name,
        )(places, *rows, down, *filled)

    early = [hidden, near, far, swapped_pair, third]
    back = project_back(early_kernel, 6, early, [], "project_out_early")
    back = project_back(late_kernel, 2, [fourth, swapped_last], [back], "project_out_late")
    back = back.reshape(groups, HALF, 2 * features)
    values = lax.all_to_all(back, "ep", split_axis=0, concat_axis=0, tiled=True)
    mixed = pl.pallas_call(
        mix_kernel,
        out_shape=jax.ShapeDtypeStruct((features, count), bf16),
        in_specs=[VMEM] * 2,
        out_specs=VMEM,
        compiler_params=LIMIT,
        cost_estimate=cost(8 * count * experts * HALF * 2 * features, 3000000),
        name="mix_rows",
    )(weigh, values.reshape(experts * HALF, 2 * features))
    return mixed.T


def solution(mesh):
    placed = (
        P("ep", "dp"),
        P("ep", None),
        P("ep", None),
        P(),
        P(),
        P("ep", "dp", None),
        P("ep", "dp", None),
        P("ep", None, "dp"),
    )
    return jax.shard_map(
        on_device, mesh=mesh, in_specs=placed, out_specs=P("ep", "dp"), check_vma=False
    )
```

```python
import functools

import jax
import jax.numpy as jnp
from jax import lax
from jax.experimental import pallas as pl
from jax.experimental.pallas import tpu as pltpu
from jax.sharding import PartitionSpec as P

HALF = 24
HELD = 20
PIECES = 4
STRIP = 256

VMEM = pl.BlockSpec(memory_space=pltpu.VMEM)
SMEM = pl.BlockSpec(memory_space=pltpu.SMEM)
NT = (((1,), (1,)), ((), ()))
HBM = pl.BlockSpec(memory_space=pltpu.HBM)
LIMIT = pltpu.CompilerParams(vmem_limit_bytes=40 * 1024 * 1024)
LARGE = pltpu.CompilerParams(vmem_limit_bytes=60 * 1024 * 1024)


def column(row, experts):
    first = lax.broadcasted_iota(jnp.int32, (experts, experts), 0)
    second = lax.broadcasted_iota(jnp.int32, (experts, experts), 1)
    spread = jnp.where(first == second, jnp.broadcast_to(row, (experts, experts)), 0.0)
    return jnp.sum(spread, axis=1, keepdims=True)


def ranks(routes, capacity, spill):
    experts = capacity.shape[1]
    top, tokens = routes.shape
    number = lax.broadcasted_iota(jnp.int32, (experts, tokens), 0)
    named = jnp.zeros((experts, tokens), jnp.float32)
    for k in range(top):
        named = named + jnp.where(routes[k : k + 1, :] == number, 1.0, 0.0)
    earlier = lax.broadcasted_iota(jnp.int32, (tokens, tokens), 0) < lax.broadcasted_iota(
        jnp.int32, (tokens, tokens), 1
    )
    before = jnp.dot(
        named.astype(jnp.bfloat16),
        jnp.where(earlier, 1.0, 0.0).astype(jnp.bfloat16),
        preferred_element_type=jnp.float32,
    )
    limit = column((capacity + spill).astype(jnp.float32), experts)
    return jnp.where((named > 0.0) & (before < limit), before, -1.0)


def pick_kernel(routes, capacity, spill, tokens, rows, named, limits, features, held, sem):
    copies = [
        pltpu.make_async_copy(routes, named, sem.at[0]),
        pltpu.make_async_copy(capacity, limits.at[0:1], sem.at[1]),
        pltpu.make_async_copy(spill, limits.at[1:2], sem.at[2]),
        pltpu.make_async_copy(tokens, features, sem.at[3]),
    ]
    for copy in copies:
        copy.start()
    for copy in copies[:3]:
        copy.wait()
    rank = ranks(named[...], limits[0:1, :], limits[1:2, :])
    experts, count = rank.shape
    slot = lax.broadcasted_iota(jnp.int32, (experts, HALF, count), 1).astype(jnp.float32)
    copies[3].wait()
    width = features.shape[0]
    group = experts // PIECES
    piece = group * HALF
    stores = []
    for k in range(PIECES):
        at = pl.ds(k * piece, piece)
        ranked = rank[k * group : (k + 1) * group][:, None, :]
        for half in range(2):
            chosen = jnp.where(ranked == slot[:group] + half * HALF, 1.0, 0.0)
            picked = lax.dot_general(
                chosen.reshape(piece, count).astype(jnp.bfloat16),
                features[...],
                NT,
                preferred_element_type=jnp.float32,
            )
            held[at, half * width : (half + 1) * width] = picked.astype(jnp.bfloat16)
        stores.append(pltpu.make_async_copy(held.at[at], rows.at[at], sem.at[4 + k]))
        stores[-1].start()
    for copy in stores:
        copy.wait()


def weigh_kernel(routes, weights, capacity, spill, weigh):
    rank = ranks(routes[...], capacity[...], spill[...])
    experts, count = rank.shape
    value = weights[...].astype(jnp.float32)
    share = value / jnp.sum(value, axis=0, keepdims=True)
    number = lax.broadcasted_iota(jnp.int32, (experts, count), 0)
    share_of = jnp.zeros((experts, count), jnp.float32)
    for k in range(value.shape[0]):
        share_of = share_of + jnp.where(routes[k : k + 1, :] == number, share[k : k + 1, :], 0.0)
    slot = lax.broadcasted_iota(jnp.int32, (experts, HALF, count), 1).astype(jnp.float32)
    for half in range(2):
        table = jnp.where(rank[:, None, :] == slot + half * HALF, share_of[:, None, :], 0.0)
        table = table.reshape(experts * HALF, count).T
        upper = table.astype(jnp.bfloat16)
        lower = (table - upper.astype(jnp.float32)).astype(jnp.bfloat16)
        weigh[half, 0:count, :] = upper
        weigh[half, count : 2 * count, :] = lower


def gather_kernel(gate, gate_other, up, up_other, weights, held, came, went):
    loads, stores = [], []
    for n, source in enumerate((gate, gate_other, up, up_other)):
        loads.append(pltpu.make_async_copy(source, held.at[n], came.at[n]))
        loads[-1].start()
    for n, load in enumerate(loads):
        load.wait()
        stores.append(pltpu.make_async_copy(held.at[n], weights.at[n], went.at[n]))
        stores[-1].start()
    for store in stores:
        store.wait()


def held_rows(chip, part):
    return part // 2 if chip in (0, 4) else part


def order_kernel(rows, after, same):
    del rows, after, same


def load_kernel(weights, weight, came):
    features = weights.shape[1]
    copies = []
    for strip in range(weight.shape[0]):
        for n, (low, kind) in enumerate(((0, 0), (1, 0), (0, 1), (1, 1))):
            copies.append(
                pltpu.make_async_copy(
                    weights.at[n, :, pl.ds(strip * STRIP, STRIP)],
                    weight.at[strip, pl.ds(low * features, features), pl.ds(kind * STRIP, STRIP)],
                    came.at[4 * strip + n],
                )
            )
    for copy in copies:
        copy.start()
    for copy in copies:
        copy.wait()


def project_kernel(places, rows, taken, weight, *refs, chips, part):
    outs, picked = refs[:-1], refs[-1]
    features = rows.shape[1] // 2
    low = 0
    for chip in chips:
        size = held_rows(chip, part)
        start = pl.multiple_of(places[chip], part // 2)
        own = rows[pl.ds(start, size), :]
        other = taken[pl.ds(start, size), :]
        for half in range(2):
            at = slice(low, low + size)
            lanes = slice(half * features, (half + 1) * features)
            picked[at, 0:features] = own[:, lanes]
            picked[at, features : 2 * features] = other[:, lanes]
            low += size
    for strip in range(weight.shape[0]):
        value = jnp.dot(picked[...], weight[strip], preferred_element_type=jnp.float32)
        value = value.astype(jnp.bfloat16)
        low = 0
        for chip, out in zip(chips, outs):
            size = 2 * held_rows(chip, part)
            out[:, strip * 2 * STRIP : (strip + 1) * 2 * STRIP] = value[low : low + size]
            low += size


def add_kernel(core, first, second, half, total):
    size = half.shape[0] // 2
    low = core[0] == 0
    for n in range(2):
        for blocks in range(2):
            at = slice((2 * n + blocks) * size, (2 * n + blocks + 1) * size)
            value = first[at, :].astype(jnp.float32) + second[at, :].astype(jnp.float32)
            more = half[n * size : (n + 1) * size, :].astype(jnp.float32)
            mine = low if blocks == 0 else jnp.logical_not(low)
            total[at, :] = jnp.where(mine, value + more, value).astype(jnp.bfloat16)


def hidden_kernel(*refs):
    terms, hidden = refs[:-1], refs[-1]
    for strip in range(hidden.shape[1] // STRIP):
        at = 2 * STRIP * strip
        gate = jnp.zeros((hidden.shape[0], STRIP), jnp.float32)
        up = gate
        for term in terms:
            gate = gate + term[:, at : at + STRIP].astype(jnp.float32)
            up = up + term[:, at + STRIP : at + 2 * STRIP].astype(jnp.float32)
        value = gate / (1.0 + jnp.exp(-gate)) * up
        hidden[:, STRIP * strip : STRIP * (strip + 1)] = value.astype(jnp.bfloat16)


def down_kernel(places, parts, down, out, held, sem, first):
    depth = held.shape[1]
    features = down.shape[0]
    copies = []
    for part, chips in parts:
        value = lax.dot_general(part, down[...], NT, preferred_element_type=jnp.float32)
        value = value.astype(jnp.bfloat16)
        for n, chip in enumerate(chips):
            low = value[2 * n * depth : (2 * n + 1) * depth]
            high = value[(2 * n + 1) * depth : (2 * n + 2) * depth]
            swapped = places[1, chip] == 1
            slot = chip - first
            held[slot, :, 0:features] = jnp.where(swapped, high, low)
            held[slot, :, features : 2 * features] = jnp.where(swapped, low, high)
            place = pl.multiple_of(places[0, chip] * depth, depth)
            copies.append(
                pltpu.make_async_copy(held.at[slot], out.at[pl.ds(place, depth)], sem.at[slot])
            )
            copies[-1].start()
    for copy in copies:
        copy.wait()


def early_kernel(places, own, near, far, swapped_pair, third, down, out, held, sem):
    rows = [term[...] for term in (own, near, far, swapped_pair, third)]
    rows = jnp.concatenate(rows, axis=0)
    down_kernel(places, ((rows, (0, 1, 2, 3, 4, 5)),), down, out, held, sem, 0)


def late_kernel(places, fourth, swapped, down, filled, out, held, sem):
    del filled
    depth = fourth.shape[0]
    rows = jnp.concatenate(
        [swapped[0 : 2 * depth], fourth[...], swapped[2 * depth : 3 * depth]], axis=0
    )
    down_kernel(places, ((rows, (6, 7)),), down, out, held, sem, 6)


def mix_kernel(weigh, values, mixed):
    features, count = mixed.shape
    width = values.shape[1]
    tiles = -(-features // 128) * 128
    total = jnp.zeros((features, count), jnp.float32)
    for half, low in enumerate((0, width - tiles)):
        part = jnp.dot(
            weigh[half], values[:, low : low + tiles], preferred_element_type=jnp.float32
        )
        part = (part[:count] + part[count:]).T
        at = half * features - low
        total = total + part[at : at + features]
    mixed[...] = total.astype(jnp.bfloat16)


def cost(flops, moved):
    return pl.CostEstimate(flops=flops, bytes_accessed=moved, transcendentals=0)


def on_device(
    tokens, routes, weights_int, capacity, spill_size, gate_weight, up_weight, down_weight
):
    experts = capacity.shape[0]
    groups = lax.axis_size("ep")
    planes = lax.axis_size("dp") // 2
    count, features = tokens.shape
    units = gate_weight.shape[2]
    bf16 = jnp.bfloat16
    core = (lax.axis_index("dp") % 2).astype(jnp.int32).reshape(1)
    swap = [(i, i ^ 1) for i in range(2 * planes)]

    own_tokens = tokens.T
    own_routes = routes.T
    own_weights = weights_int.T
    cap_row = capacity.reshape(1, experts)
    spill_row = spill_size.reshape(1, experts)
    gate = gate_weight[0]
    up = up_weight[0]
    down = down_weight[0].T

    gate_other = lax.ppermute(gate, "dp", swap)
    up_other = lax.ppermute(up, "dp", swap)

    send = pl.pallas_call(
        pick_kernel,
        out_shape=jax.ShapeDtypeStruct((experts * HALF, 2 * features), bf16),
        in_specs=[HBM] * 4,
        out_specs=HBM,
        scratch_shapes=[
            pltpu.VMEM(own_routes.shape, jnp.int32),
            pltpu.VMEM((2, experts), jnp.int32),
            pltpu.VMEM((features, count), bf16),
            pltpu.VMEM((experts * HALF, 2 * features), bf16),
            pltpu.SemaphoreType.DMA((4 + PIECES,)),
        ],
        compiler_params=pltpu.CompilerParams(vmem_limit_bytes=60 * 1024 * 1024),
        cost_estimate=cost(2 * experts * HALF * count * 2 * features, 2000000),
        name="pick_rows",
    )(own_routes, cap_row, spill_row, own_tokens)
    got = lax.all_to_all(
        send.reshape(groups, HALF, 2 * features), "ep", split_axis=0, concat_axis=0, tiled=True
    ).reshape(groups * HALF, 2 * features)

    depth = groups * HALF
    weights = pl.pallas_call(
        gather_kernel,
        out_shape=jax.ShapeDtypeStruct((HELD,) + gate.shape, bf16),
        in_specs=[HBM] * 4,
        out_specs=HBM,
        scratch_shapes=[
            pltpu.VMEM((4,) + gate.shape, bf16),
            pltpu.SemaphoreType.DMA((4,)),
            pltpu.SemaphoreType.DMA((4,)),
        ],
        compiler_params=LIMIT,
        cost_estimate=cost(0, 7400000),
        name="gather_weights",
    )(gate, gate_other, up, up_other)
    strips = units // STRIP
    part = depth // planes
    plane = lax.axis_index("dp") // 2
    sense = 1 - 2 * core[0]

    places = jnp.stack(
        [
            (plane + sense * k + planes) % planes * part + (core[0] * part // 2 if k in (0, 4) else 0)
            for k in range(5)
        ]
    ).astype(jnp.int32)
    anywhere = pl.BlockSpec(memory_space=pl.ANY)
    got = pl.pallas_call(
        order_kernel,
        out_shape=jax.ShapeDtypeStruct(got.shape, bf16),
        in_specs=[anywhere] * 2,
        out_specs=anywhere,
        input_output_aliases={0: 0},
        compiler_params=LIMIT,
        cost_estimate=cost(0, 1000),
        name="after_weights",
    )(got, weights)
    taken = lax.ppermute(got, "dp", swap)
    weight = pl.pallas_call(
        load_kernel,
        out_shape=jax.ShapeDtypeStruct((strips, 2 * features, 2 * STRIP), bf16),
        in_specs=[HBM],
        out_specs=VMEM,
        scratch_shapes=[pltpu.SemaphoreType.DMA((4 * strips,))],
        compiler_params=pltpu.CompilerParams(vmem_limit_bytes=48 * 1024 * 1024),
        cost_estimate=cost(0, 7400000),
        name="load_weights",
    )(weights)

    def project(chips, name):
        sizes = [2 * held_rows(chip, part) for chip in chips]
        return pl.pallas_call(
            functools.partial(project_kernel, chips=chips, part=part),
            out_shape=[jax.ShapeDtypeStruct((size, 2 * units), bf16) for size in sizes],
            in_specs=[SMEM] + [VMEM] * 3,
            out_specs=[VMEM] * len(sizes),
            scratch_shapes=[pltpu.VMEM((sum(sizes), 2 * features), bf16)],
            compiler_params=LIMIT,
            cost_estimate=cost(2 * sum(sizes) * 2 * features * 2 * units, 6000000),
            name=name,
        )(places, got, taken, weight)

    def flow(rows, hops):
        steps = [
            (2 * z + c, 2 * ((z + (hops, -hops)[c]) % planes) + c)
            for z in range(planes)
            for c in range(2)
        ]
        return lax.ppermute(rows, "dp", steps)

    def add(first, second, half, name):
        return pl.pallas_call(
            add_kernel,
            out_shape=jax.ShapeDtypeStruct((2 * part, 2 * units), bf16),
            in_specs=[SMEM] + [VMEM] * 3,
            out_specs=VMEM,
            compiler_params=LIMIT,
            cost_estimate=cost(6 * part * units, 3000000),
            name=name,
        )(core, first, second, half)

    (fourth,) = project((4,), "project_in_opposite")
    (third,) = project((3,), "project_in_third")
    second, first, here = project((2, 1, 0), "project_in_near")
    second = add(second, flow(third, 1), flow(fourth, 2), "add_passing")
    reached = add(flow(first, 1), flow(second, 2), here, "add_reached")
    terms = (reached, lax.ppermute(reached, "dp", swap))
    weigh = pl.pallas_call(
        weigh_kernel,
        out_shape=jax.ShapeDtypeStruct((2, 2 * count, experts * HALF), bf16),
        in_specs=[VMEM] * 4,
        out_specs=VMEM,
        compiler_params=LIMIT,
        cost_estimate=cost(2 * experts * count * count, 4000000),
        name="weigh_table",
    )(own_routes, own_weights, cap_row, spill_row)
    hidden = pl.pallas_call(
        hidden_kernel,
        out_shape=jax.ShapeDtypeStruct((2 * part, units), bf16),
        in_specs=[VMEM] * len(terms),
        out_specs=VMEM,
        compiler_params=LIMIT,
        cost_estimate=cost(8 * part * units, 2000000),
        name="hidden_units",
    )(*terms)

    near, far = flow(hidden, 1), flow(hidden, 2)
    far_half = jnp.where(core[0] == 0, far[:part], far[part:])
    third, fourth = flow(far, 1), flow(far_half, 2)
    swapped_pair = lax.ppermute(jnp.concatenate([near, far], axis=0), "dp", swap)
    swapped_last = lax.ppermute(jnp.concatenate([third, fourth], axis=0), "dp", swap)
    offsets = [0, -sense, -2 * sense, sense, 2 * sense, -3 * sense, 3 * sense, 4]
    orders = [core[0] * 0] * 7 + [core[0]]
    places = jnp.stack(
        [jnp.stack([(plane + chip + planes) % planes for chip in offsets]), jnp.stack(orders)]
    ).astype(jnp.int32)
    back_shape = jax.ShapeDtypeStruct((depth, 2 * features), bf16)

    def scratch(held):
        return [
            pltpu.VMEM((held, part, 2 * features), bf16),
            pltpu.SemaphoreType.DMA((held,)),
        ]

    def project_back(kernel, held, rows, filled, name):
        return pl.pallas_call(
            kernel,
            out_shape=back_shape,
            in_specs=[SMEM] + [VMEM] * (len(rows) + 1) + [HBM] * len(filled),
            out_specs=HBM,
            scratch_shapes=scratch(held),
            input_output_aliases={len(rows) + 2: 0} if filled else {},
            compiler_params=LIMIT,
            cost_estimate=cost(4 * held * part * units * features, 3000000),
            name=name,
        )(places, *rows, down, *filled)

    early = [hidden, near, far, swapped_pair, third]
    back = project_back(early_kernel, 6, early, [], "project_out_early")
    back = project_back(late_kernel, 2, [fourth, swapped_last], [back], "project_out_late")
    back = back.reshape(groups, HALF, 2 * features)
    values = lax.all_to_all(back, "ep", split_axis=0, concat_axis=0, tiled=True)
    mixed = pl.pallas_call(
        mix_kernel,
        out_shape=jax.ShapeDtypeStruct((features, count), bf16),
        in_specs=[VMEM] * 2,
        out_specs=VMEM,
        compiler_params=LIMIT,
        cost_estimate=cost(8 * count * experts * HALF * 2 * features, 3000000),
        name="mix_rows",
    )(weigh, values.reshape(experts * HALF, 2 * features))
    return mixed.T


def solution(mesh):
    placed = (
        P("ep", "dp"),
        P("ep", None),
        P("ep", None),
        P(),
        P(),
        P("ep", "dp", None),
        P("ep", "dp", None),
        P("ep", None, "dp"),
    )
    return jax.shard_map(
        on_device, mesh=mesh, in_specs=placed, out_specs=P("ep", "dp"), check_vma=False
    )
```

```python
import functools

import jax
import jax.numpy as jnp
from jax import lax
from jax.experimental import pallas as pl
from jax.experimental.pallas import tpu as pltpu
from jax.sharding import PartitionSpec as P

HALF = 24
HELD = 20
PIECES = 4
STRIP = 256

VMEM = pl.BlockSpec(memory_space=pltpu.VMEM)
SMEM = pl.BlockSpec(memory_space=pltpu.SMEM)
NT = (((1,), (1,)), ((), ()))
HBM = pl.BlockSpec(memory_space=pltpu.HBM)
LIMIT = pltpu.CompilerParams(vmem_limit_bytes=40 * 1024 * 1024)
LARGE = pltpu.CompilerParams(vmem_limit_bytes=60 * 1024 * 1024)


def column(row, experts):
    first = lax.broadcasted_iota(jnp.int32, (experts, experts), 0)
    second = lax.broadcasted_iota(jnp.int32, (experts, experts), 1)
    spread = jnp.where(first == second, jnp.broadcast_to(row, (experts, experts)), 0.0)
    return jnp.sum(spread, axis=1, keepdims=True)


def ranks(routes, capacity, spill):
    experts = capacity.shape[1]
    top, tokens = routes.shape
    number = lax.broadcasted_iota(jnp.int32, (experts, tokens), 0)
    named = jnp.zeros((experts, tokens), jnp.float32)
    for k in range(top):
        named = named + jnp.where(routes[k : k + 1, :] == number, 1.0, 0.0)
    earlier = lax.broadcasted_iota(jnp.int32, (tokens, tokens), 0) < lax.broadcasted_iota(
        jnp.int32, (tokens, tokens), 1
    )
    before = jnp.dot(
        named.astype(jnp.bfloat16),
        jnp.where(earlier, 1.0, 0.0).astype(jnp.bfloat16),
        preferred_element_type=jnp.float32,
    )
    limit = column((capacity + spill).astype(jnp.float32), experts)
    return jnp.where((named > 0.0) & (before < limit), before, -1.0)


def pick_kernel(routes, capacity, spill, tokens, rows, named, limits, features, held, sem):
    copies = [
        pltpu.make_async_copy(routes, named, sem.at[0]),
        pltpu.make_async_copy(capacity, limits.at[0:1], sem.at[1]),
        pltpu.make_async_copy(spill, limits.at[1:2], sem.at[2]),
        pltpu.make_async_copy(tokens, features, sem.at[3]),
    ]
    for copy in copies:
        copy.start()
    for copy in copies[:3]:
        copy.wait()
    rank = ranks(named[...], limits[0:1, :], limits[1:2, :])
    experts, count = rank.shape
    slot = lax.broadcasted_iota(jnp.int32, (experts, HALF, count), 1).astype(jnp.float32)
    copies[3].wait()
    width = features.shape[0]
    group = experts // PIECES
    piece = group * HALF
    stores = []
    for k in range(PIECES):
        at = pl.ds(k * piece, piece)
        ranked = rank[k * group : (k + 1) * group][:, None, :]
        for half in range(2):
            chosen = jnp.where(ranked == slot[:group] + half * HALF, 1.0, 0.0)
            picked = lax.dot_general(
                chosen.reshape(piece, count).astype(jnp.bfloat16),
                features[...],
                NT,
                preferred_element_type=jnp.float32,
            )
            held[at, half * width : (half + 1) * width] = picked.astype(jnp.bfloat16)
        stores.append(pltpu.make_async_copy(held.at[at], rows.at[at], sem.at[4 + k]))
        stores[-1].start()
    for copy in stores:
        copy.wait()


def weigh_kernel(routes, weights, capacity, spill, weigh):
    rank = ranks(routes[...], capacity[...], spill[...])
    experts, count = rank.shape
    value = weights[...].astype(jnp.float32)
    share = value / jnp.sum(value, axis=0, keepdims=True)
    number = lax.broadcasted_iota(jnp.int32, (experts, count), 0)
    share_of = jnp.zeros((experts, count), jnp.float32)
    for k in range(value.shape[0]):
        share_of = share_of + jnp.where(routes[k : k + 1, :] == number, share[k : k + 1, :], 0.0)
    slot = lax.broadcasted_iota(jnp.int32, (experts, HALF, count), 1).astype(jnp.float32)
    for half in range(2):
        table = jnp.where(rank[:, None, :] == slot + half * HALF, share_of[:, None, :], 0.0)
        table = table.reshape(experts * HALF, count).T
        upper = table.astype(jnp.bfloat16)
        lower = (table - upper.astype(jnp.float32)).astype(jnp.bfloat16)
        weigh[half, 0:count, :] = upper
        weigh[half, count : 2 * count, :] = lower


def gather_kernel(gate, gate_other, up, up_other, weights, held, came, went):
    loads, stores = [], []
    for n, source in enumerate((gate, gate_other, up, up_other)):
        loads.append(pltpu.make_async_copy(source, held.at[n], came.at[n]))
        loads[-1].start()
    for n, load in enumerate(loads):
        load.wait()
        stores.append(pltpu.make_async_copy(held.at[n], weights.at[n], went.at[n]))
        stores[-1].start()
    for store in stores:
        store.wait()


def held_rows(chip, part):
    return part // 2 if chip in (0, 4) else part


def order_kernel(rows, after, same):
    del rows, after, same


def load_kernel(weights, weight, came):
    features = weights.shape[1]
    copies = []
    for strip in range(weight.shape[0]):
        for n, (low, kind) in enumerate(((0, 0), (1, 0), (0, 1), (1, 1))):
            copies.append(
                pltpu.make_async_copy(
                    weights.at[n, :, pl.ds(strip * STRIP, STRIP)],
                    weight.at[strip, pl.ds(low * features, features), pl.ds(kind * STRIP, STRIP)],
                    came.at[4 * strip + n],
                )
            )
    for copy in copies:
        copy.start()
    for copy in copies:
        copy.wait()


def project_kernel(places, rows, taken, weight, *refs, chips, part):
    outs, picked = refs[:-1], refs[-1]
    features = rows.shape[1] // 2
    low = 0
    for chip in chips:
        size = held_rows(chip, part)
        start = pl.multiple_of(places[chip], part // 2)
        own = rows[pl.ds(start, size), :]
        other = taken[pl.ds(start, size), :]
        for half in range(2):
            at = slice(low, low + size)
            lanes = slice(half * features, (half + 1) * features)
            picked[at, 0:features] = own[:, lanes]
            picked[at, features : 2 * features] = other[:, lanes]
            low += size
    for strip in range(weight.shape[0]):
        value = jnp.dot(picked[...], weight[strip], preferred_element_type=jnp.float32)
        value = value.astype(jnp.bfloat16)
        low = 0
        for chip, out in zip(chips, outs):
            size = 2 * held_rows(chip, part)
            out[:, strip * 2 * STRIP : (strip + 1) * 2 * STRIP] = value[low : low + size]
            low += size


def add_kernel(core, first, second, half, total):
    size = half.shape[0] // 2
    low = core[0] == 0
    for n in range(2):
        for blocks in range(2):
            at = slice((2 * n + blocks) * size, (2 * n + blocks + 1) * size)
            value = first[at, :].astype(jnp.float32) + second[at, :].astype(jnp.float32)
            more = half[n * size : (n + 1) * size, :].astype(jnp.float32)
            mine = low if blocks == 0 else jnp.logical_not(low)
            total[at, :] = jnp.where(mine, value + more, value).astype(jnp.bfloat16)


def hidden_kernel(*refs):
    terms, hidden = refs[:-1], refs[-1]
    for strip in range(hidden.shape[1] // STRIP):
        at = 2 * STRIP * strip
        gate = jnp.zeros((hidden.shape[0], STRIP), jnp.float32)
        up = gate
        for term in terms:
            gate = gate + term[:, at : at + STRIP].astype(jnp.float32)
            up = up + term[:, at + STRIP : at + 2 * STRIP].astype(jnp.float32)
        value = gate / (1.0 + jnp.exp(-gate)) * up
        hidden[:, STRIP * strip : STRIP * (strip + 1)] = value.astype(jnp.bfloat16)


def down_kernel(places, parts, down, out, held, sem, first):
    depth = held.shape[1]
    features = down.shape[0]
    copies = []
    for part, chips in parts:
        value = lax.dot_general(part, down[...], NT, preferred_element_type=jnp.float32)
        value = value.astype(jnp.bfloat16)
        for n, chip in enumerate(chips):
            low = value[2 * n * depth : (2 * n + 1) * depth]
            high = value[(2 * n + 1) * depth : (2 * n + 2) * depth]
            swapped = places[1, chip] == 1
            slot = chip - first
            held[slot, :, 0:features] = jnp.where(swapped, high, low)
            held[slot, :, features : 2 * features] = jnp.where(swapped, low, high)
            place = pl.multiple_of(places[0, chip] * depth, depth)
            copies.append(
                pltpu.make_async_copy(held.at[slot], out.at[pl.ds(place, depth)], sem.at[slot])
            )
            copies[-1].start()
    for copy in copies:
        copy.wait()


def early_kernel(places, own, near, far, swapped_pair, third, down, out, held, sem):
    rows = [term[...] for term in (own, near, far, swapped_pair, third)]
    rows = jnp.concatenate(rows, axis=0)
    down_kernel(places, ((rows, (0, 1, 2, 3, 4, 5)),), down, out, held, sem, 0)


def late_kernel(places, fourth, swapped, down, filled, out, held, sem):
    del filled
    depth = fourth.shape[0]
    rows = jnp.concatenate(
        [swapped[0 : 2 * depth], fourth[...], swapped[2 * depth : 3 * depth]], axis=0
    )
    down_kernel(places, ((rows, (6, 7)),), down, out, held, sem, 6)


def mix_kernel(weigh, values, mixed):
    features, count = mixed.shape
    width = values.shape[1]
    tiles = -(-features // 128) * 128
    total = jnp.zeros((features, count), jnp.float32)
    for half, low in enumerate((0, width - tiles)):
        part = jnp.dot(
            weigh[half], values[:, low : low + tiles], preferred_element_type=jnp.float32
        )
        part = (part[:count] + part[count:]).T
        at = half * features - low
        total = total + part[at : at + features]
    mixed[...] = total.astype(jnp.bfloat16)


def cost(flops, moved):
    return pl.CostEstimate(flops=flops, bytes_accessed=moved, transcendentals=0)


def on_device(
    tokens, routes, weights_int, capacity, spill_size, gate_weight, up_weight, down_weight
):
    experts = capacity.shape[0]
    groups = lax.axis_size("ep")
    planes = lax.axis_size("dp") // 2
    count, features = tokens.shape
    units = gate_weight.shape[2]
    bf16 = jnp.bfloat16
    core = (lax.axis_index("dp") % 2).astype(jnp.int32).reshape(1)
    swap = [(i, i ^ 1) for i in range(2 * planes)]

    own_tokens = tokens.T
    own_routes = routes.T
    own_weights = weights_int.T
    cap_row = capacity.reshape(1, experts)
    spill_row = spill_size.reshape(1, experts)
    gate = gate_weight[0]
    up = up_weight[0]
    down = down_weight[0].T

    gate_other = lax.ppermute(gate, "dp", swap)
    up_other = lax.ppermute(up, "dp", swap)

    send = pl.pallas_call(
        pick_kernel,
        out_shape=jax.ShapeDtypeStruct((experts * HALF, 2 * features), bf16),
        in_specs=[HBM] * 4,
        out_specs=HBM,
        scratch_shapes=[
            pltpu.VMEM(own_routes.shape, jnp.int32),
            pltpu.VMEM((2, experts), jnp.int32),
            pltpu.VMEM((features, count), bf16),
            pltpu.VMEM((experts * HALF, 2 * features), bf16),
            pltpu.SemaphoreType.DMA((4 + PIECES,)),
        ],
        compiler_params=pltpu.CompilerParams(vmem_limit_bytes=60 * 1024 * 1024),
        cost_estimate=cost(2 * experts * HALF * count * 2 * features, 2000000),
        name="pick_rows",
    )(own_routes, cap_row, spill_row, own_tokens)
    got = lax.all_to_all(
        send.reshape(groups, HALF, 2 * features), "ep", split_axis=0, concat_axis=0, tiled=True
    ).reshape(groups * HALF, 2 * features)

    depth = groups * HALF
    weights = pl.pallas_call(
        gather_kernel,
        out_shape=jax.ShapeDtypeStruct((HELD,) + gate.shape, bf16),
        in_specs=[HBM] * 4,
        out_specs=HBM,
        scratch_shapes=[
            pltpu.VMEM((4,) + gate.shape, bf16),
            pltpu.SemaphoreType.DMA((4,)),
            pltpu.SemaphoreType.DMA((4,)),
        ],
        compiler_params=LIMIT,
        cost_estimate=cost(0, 7400000),
        name="gather_weights",
    )(gate, gate_other, up, up_other)
    strips = units // STRIP
    part = depth // planes
    plane = lax.axis_index("dp") // 2
    sense = 1 - 2 * core[0]

    places = jnp.stack(
        [
            (plane + sense * k + planes) % planes * part + (core[0] * part // 2 if k in (0, 4) else 0)
            for k in range(5)
        ]
    ).astype(jnp.int32)
    anywhere = pl.BlockSpec(memory_space=pl.ANY)
    got = pl.pallas_call(
        order_kernel,
        out_shape=jax.ShapeDtypeStruct(got.shape, bf16),
        in_specs=[anywhere] * 2,
        out_specs=anywhere,
        input_output_aliases={0: 0},
        compiler_params=LIMIT,
        cost_estimate=cost(0, 1000),
        name="after_weights",
    )(got, weights)
    taken = lax.ppermute(got, "dp", swap)
    weight = pl.pallas_call(
        load_kernel,
        out_shape=jax.ShapeDtypeStruct((strips, 2 * features, 2 * STRIP), bf16),
        in_specs=[HBM],
        out_specs=VMEM,
        scratch_shapes=[pltpu.SemaphoreType.DMA((4 * strips,))],
        compiler_params=pltpu.CompilerParams(vmem_limit_bytes=48 * 1024 * 1024),
        cost_estimate=cost(0, 7400000),
        name="load_weights",
    )(weights)

    def project(chips, name):
        sizes = [2 * held_rows(chip, part) for chip in chips]
        return pl.pallas_call(
            functools.partial(project_kernel, chips=chips, part=part),
            out_shape=[jax.ShapeDtypeStruct((size, 2 * units), bf16) for size in sizes],
            in_specs=[SMEM] + [VMEM] * 3,
            out_specs=[VMEM] * len(sizes),
            scratch_shapes=[pltpu.VMEM((sum(sizes), 2 * features), bf16)],
            compiler_params=LIMIT,
            cost_estimate=cost(2 * sum(sizes) * 2 * features * 2 * units, 6000000),
            name=name,
        )(places, got, taken, weight)

    def flow(rows, hops):
        steps = [
            (2 * z + c, 2 * ((z + (hops, -hops)[c]) % planes) + c)
            for z in range(planes)
            for c in range(2)
        ]
        return lax.ppermute(rows, "dp", steps)

    def add(first, second, half, name):
        return pl.pallas_call(
            add_kernel,
            out_shape=jax.ShapeDtypeStruct((2 * part, 2 * units), bf16),
            in_specs=[SMEM] + [VMEM] * 3,
            out_specs=VMEM,
            compiler_params=LIMIT,
            cost_estimate=cost(6 * part * units, 3000000),
            name=name,
        )(core, first, second, half)

    (fourth,) = project((4,), "project_in_opposite")
    (third,) = project((3,), "project_in_third")
    (first,) = project((1,), "project_in_first")
    second, here = project((2, 0), "project_in_second")
    second = add(second, flow(third, 1), flow(fourth, 2), "add_passing")
    reached = add(flow(first, 1), flow(second, 2), here, "add_reached")
    terms = (reached, lax.ppermute(reached, "dp", swap))
    weigh = pl.pallas_call(
        weigh_kernel,
        out_shape=jax.ShapeDtypeStruct((2, 2 * count, experts * HALF), bf16),
        in_specs=[VMEM] * 4,
        out_specs=VMEM,
        compiler_params=LIMIT,
        cost_estimate=cost(2 * experts * count * count, 4000000),
        name="weigh_table",
    )(own_routes, own_weights, cap_row, spill_row)
    hidden = pl.pallas_call(
        hidden_kernel,
        out_shape=jax.ShapeDtypeStruct((2 * part, units), bf16),
        in_specs=[VMEM] * len(terms),
        out_specs=VMEM,
        compiler_params=LIMIT,
        cost_estimate=cost(8 * part * units, 2000000),
        name="hidden_units",
    )(*terms)

    near, far = flow(hidden, 1), flow(hidden, 2)
    far_half = jnp.where(core[0] == 0, far[:part], far[part:])
    third, fourth = flow(far, 1), flow(far_half, 2)
    swapped_pair = lax.ppermute(jnp.concatenate([near, far], axis=0), "dp", swap)
    swapped_last = lax.ppermute(jnp.concatenate([third, fourth], axis=0), "dp", swap)
    offsets = [0, -sense, -2 * sense, sense, 2 * sense, -3 * sense, 3 * sense, 4]
    orders = [core[0] * 0] * 7 + [core[0]]
    places = jnp.stack(
        [jnp.stack([(plane + chip + planes) % planes for chip in offsets]), jnp.stack(orders)]
    ).astype(jnp.int32)
    back_shape = jax.ShapeDtypeStruct((depth, 2 * features), bf16)

    def scratch(held):
        return [
            pltpu.VMEM((held, part, 2 * features), bf16),
            pltpu.SemaphoreType.DMA((held,)),
        ]

    def project_back(kernel, held, rows, filled, name):
        return pl.pallas_call(
            kernel,
            out_shape=back_shape,
            in_specs=[SMEM] + [VMEM] * (len(rows) + 1) + [HBM] * len(filled),
            out_specs=HBM,
            scratch_shapes=scratch(held),
            input_output_aliases={len(rows) + 2: 0} if filled else {},
            compiler_params=LIMIT,
            cost_estimate=cost(4 * held * part * units * features, 3000000),
            name=name,
        )(places, *rows, down, *filled)

    early = [hidden, near, far, swapped_pair, third]
    back = project_back(early_kernel, 6, early, [], "project_out_early")
    back = project_back(late_kernel, 2, [fourth, swapped_last], [back], "project_out_late")
    back = back.reshape(groups, HALF, 2 * features)
    values = lax.all_to_all(back, "ep", split_axis=0, concat_axis=0, tiled=True)
    mixed = pl.pallas_call(
        mix_kernel,
        out_shape=jax.ShapeDtypeStruct((features, count), bf16),
        in_specs=[VMEM] * 2,
        out_specs=VMEM,
        compiler_params=LIMIT,
        cost_estimate=cost(8 * count * experts * HALF * 2 * features, 3000000),
        name="mix_rows",
    )(weigh, values.reshape(experts * HALF, 2 * features))
    return mixed.T


def solution(mesh):
    placed = (
        P("ep", "dp"),
        P("ep", None),
        P("ep", None),
        P(),
        P(),
        P("ep", "dp", None),
        P("ep", "dp", None),
        P("ep", None, "dp"),
    )
    return jax.shard_map(
        on_device, mesh=mesh, in_specs=placed, out_specs=P("ep", "dp"), check_vma=False
    )
```
